128 devices in a mesh: band: 8 (over y_hi, x), domain: 16 (over y_lo, z, core).
Axes of the slice: x: 4, y: 4 (y_hi: 2, y_lo: 2; y = y_hi * 2 + y_lo), z: 4, core: 2. Of those that a mesh axis runs over, the one named last changes fastest.
Arguments:
- orbitals: bfloat16 [128, 128, 64, 128], P('band', 'domain'), may hold values from -20 to 20, as said below
- potential: float32 [128, 64, 128], P('domain'), may hold values from 0 to 3
Outputs:
- correlation: float32 [128, 128], P('band')
- projected: float32 [128, 128], P('band')
The draws below stay inside these ranges and needn't reach their ends.
Inputs may be any that keep to these rules, and one draw needn't show every extreme that they name: real-valued trial orbitals.
All inputs are finite; a program needn't handle non-finite values.
Results may differ from the reference program's by a relative error of at most 0.00049.
Values may be sent and summed in bfloat16 or wider, within the bound.
No kernel may reach another device: no remote copies, remote signals or barrier semaphores. Data moves between devices by JAX's collectives and lax.ppermute only.
A program may use at most 128 MiB of HBM per device.

```python
import jax
import jax.numpy as jnp
from jax import lax

ORB_DEV = 16
NY = 64
NZ = 128
NORB = 128
NX = 128
N_BAND = 8


def box_profile(key, rows, length, lowest, highest):
    wave_counts = jax.random.randint(key, (rows, 4), lowest, highest + 1).astype(jnp.float32)
    positions = (jnp.arange(length, dtype=jnp.float32) + 0.5) / length
    return jnp.sin(jnp.pi * wave_counts[:, :, None] * positions[None, None, :])


def draw_orbitals(key, part):
    key = jax.random.fold_in(key, 11)
    key_noise = jax.random.fold_in(key, 0)
    key_shared = jax.random.fold_in(key, 1)
    key_mix = jax.random.fold_in(key, 2)
    key_modes = jax.random.fold_in(key, 4)
    key_amps = jax.random.fold_in(key, 5)
    shape = (NORB, NX, NY, NZ)
    noise = jax.random.normal(key_noise, shape, jnp.float32)
    mixing = 0.45 * jax.random.normal(key_mix, (NORB, 8), jnp.float32)
    total = noise
    for index in range(8):
        shared = jax.random.normal(jax.random.fold_in(key_shared, index), (NX, NY, NZ), jnp.float32)
        total = total + mixing[:, index][:, None, None, None] * shared[None]
    along_x = box_profile(jax.random.fold_in(key_modes, 0), NORB, NX, 1, 4)
    along_y = box_profile(jax.random.fold_in(key_modes, 1), NORB, NY, 1, 4)
    along_z = box_profile(jax.random.fold_in(key_modes, 2), NORB, NZ, 1, 4)
    weights = 2.5 * jax.random.normal(key_amps, (NORB, 4), jnp.float32)
    for index in range(4):
        smooth_part = along_x[:, index][:, :, None, None] * along_y[:, index][:, None, :, None] * along_z[:, index][:, None, None, :]
        total = total + weights[:, index][:, None, None, None] * smooth_part
    total = jnp.clip(total, -12.0, 12.0)
    ramp = 0.6 + jnp.arange(NX, dtype=jnp.float32) / NX
    return (total * ramp[None, :, None, None]).astype(jnp.bfloat16)


def draw_potential(key, part):
    key = jax.random.fold_in(key, 23)
    return jax.random.uniform(key, (NX, NY, NZ), jnp.float32, 0.0, 3.0)


def setup_inputs(seed: int = 0) -> dict:
    arg_keys = jax.random.split(jax.random.key(seed), 3)
    return {
        "orbitals": draw_orbitals(jax.random.fold_in(arg_keys[2], 71), 0),
        "potential": draw_potential(jax.random.fold_in(arg_keys[2], 71), 0),
    }


COEFS = (-5369.0 / 1800.0, 12.0 / 7.0, -15.0 / 56.0, 10.0 / 189.0, -1.0 / 112.0, 2.0 / 1925.0, -1.0 / 16632.0)
CENTER = 8.0
HALF = 5.0


def apply_ham(field, potential):
    count, nx, ny, nz = field.shape
    wide = jnp.pad(field.astype(jnp.float32), ((0, 0), (6, 6), (6, 6), (6, 6)))
    center = wide[:, 6:6 + nx, 6:6 + ny, 6:6 + nz]
    lap = 3.0 * COEFS[0] * center
    for s in range(1, 7):
        near = wide[:, 6 + s:6 + s + nx, 6:6 + ny, 6:6 + nz] + wide[:, 6 - s:6 - s + nx, 6:6 + ny, 6:6 + nz]
        near = near + wide[:, 6:6 + nx, 6 + s:6 + s + ny, 6:6 + nz] + wide[:, 6:6 + nx, 6 - s:6 - s + ny, 6:6 + nz]
        near = near + wide[:, 6:6 + nx, 6:6 + ny, 6 + s:6 + s + nz] + wide[:, 6:6 + nx, 6:6 + ny, 6 - s:6 - s + nz]
        lap = lap + COEFS[s] * near
    return -0.5 * lap + potential[None] * center, center


def filter_block(block, potential):
    hx, xc = apply_ham(block, potential)
    first = ((hx - CENTER * xc) / HALF).astype(jnp.bfloat16)
    hf, fc = apply_ham(first, potential)
    filtered = (2.0 * (hf - CENTER * fc) / HALF - xc).astype(jnp.bfloat16)
    happ, unused = apply_ham(filtered, potential)
    return filtered, happ.astype(jnp.bfloat16)


def reference(orbitals, potential):
    blocks = orbitals.reshape((N_BAND, ORB_DEV, NX, NY, NZ))
    filtered, applied = lax.map(lambda blk: filter_block(blk, potential), blocks)
    flat_f = filtered.reshape((NORB, NX * NY * NZ))
    flat_a = applied.reshape((NORB, NX * NY * NZ))
    cells = float(NX * NY * NZ)
    correlation = lax.dot_general(flat_f, flat_f, (((1,), (1,)), ((), ())), preferred_element_type=jnp.float32) / cells
    projected = lax.dot_general(flat_a, flat_f, (((1,), (1,)), ((), ())), preferred_element_type=jnp.float32) / cells
    return correlation, projected
```

```python
import functools

import jax
import jax.numpy as jnp
import ml_dtypes
import numpy as np
from jax import lax
from jax.experimental import pallas as pl
from jax.experimental.pallas import tpu as pltpu
from jax.sharding import PartitionSpec as P

COEFS = (
    -5369.0 / 1800.0,
    12.0 / 7.0,
    -15.0 / 56.0,
    10.0 / 189.0,
    -1.0 / 112.0,
    2.0 / 1925.0,
    -1.0 / 16632.0,
)
CENTER = 8.0
HALF = 5.0
REACH = 6
SIDE = tuple(-0.5 * c / HALF for c in COEFS)
BF16 = jnp.bfloat16
F32 = jnp.float32
ORBS_STEP = 2
ROWS = 16


def band_matrix(size):
    index = np.arange(size)
    gap = np.abs(index[:, None] - index[None, :])
    weights = np.array([0.0] + list(SIDE[1:]))
    return np.where(gap <= REACH, weights[np.minimum(gap, REACH)], 0.0)


def split_two(matrix):
    high = matrix.astype(ml_dtypes.bfloat16)
    low = (matrix - high.astype(np.float64)).astype(ml_dtypes.bfloat16)
    return high, low


def stencil_matrices(ny, nz, planes):
    high, low = split_two(band_matrix(nz))
    along_z = np.concatenate([high, low], axis=0)
    high, low = split_two(np.kron(np.eye(planes), band_matrix(ny)))
    along_y = np.concatenate([high, low], axis=1)
    return along_z, along_y


def stage_body(stage, width, planes, *refs):
    if stage == 2:
        c_ref, on_ref, off_ref, v_ref, mz_ref, my_ref, o_ref = refs[:7]
        outs = refs[7:]
    else:
        c_ref, on_ref, off_ref, v_ref, mz_ref, my_ref = refs[:6]
        outs = refs[6:]
    nx, orbs, ny, nz = c_ref.shape
    group = my_ref.shape[0] // ny
    for b in range(orbs):
        flat = c_ref[:, b].reshape(nx * ny, nz)
        z_term = jnp.dot(
            jnp.concatenate([flat, flat], axis=1), mz_ref[...], preferred_element_type=F32
        ).reshape(nx, ny, nz)
        y_parts = []
        for q in range(0, nx, group):
            part = c_ref[q : q + group, b].reshape(group * ny, nz)
            y_parts.append(
                jnp.dot(
                    my_ref[...],
                    jnp.concatenate([part, part], axis=0),
                    preferred_element_type=F32,
                ).reshape(group, ny, nz)
            )
        for r in range(0, ny, ROWS):
            rows = slice(r, r + ROWS)
            wide = {}
            for p in range(nx):
                wide[p] = c_ref[p, b, rows].astype(F32)
            for i in range(width):
                wide[-1 - i] = off_ref[i, b, rows].astype(F32)
                wide[nx + i] = on_ref[width - 1 - i, b, rows].astype(F32)
            for p in range(nx):
                total = (
                    v_ref[p, rows] * wide[p]
                    + z_term[p, rows]
                    + y_parts[p // group][p % group, rows]
                )
                for s in range(1, REACH + 1):
                    low, high = p - s, p + s
                    near = []
                    twice = []
                    for q, gap in ((low, p), (high, nx - 1 - p)):
                        if q not in wide:
                            continue
                        outside = q < 0 or q >= nx
                        if outside and width < REACH and gap >= width:
                            twice.append(wide[q])
                        else:
                            near.append(wide[q])
                    if near:
                        total = total + SIDE[s] * sum(near[1:], near[0])
                    if twice:
                        total = total + (2.0 * SIDE[s]) * sum(twice[1:], twice[0])
                if stage == 2:
                    total = 2.0 * total - o_ref[p, b, rows].astype(F32)
                elif stage == 3:
                    total = HALF * total + CENTER * wide[p]
                result = total.astype(BF16)
                outs[0][p, b, rows] = result
                if stage < 3:
                    keep = planes
                    if p >= nx - keep:
                        outs[1][p - (nx - keep), b, rows] = result
                    if p < keep:
                        outs[2][p, b, rows] = result


def run_stage(stage, field, on, off, shifted, along_z, along_y, orbitals=None):
    nx, orbs, ny, nz = field.shape
    width = on.shape[0]
    send = {1: REACH, 2: REACH // 2, 3: 0}[stage]
    step = ORBS_STEP

    def planes_spec(count):
        return pl.BlockSpec((count, step, ny, nz), lambda i: (0, i, 0, 0))

    def whole(array):
        return pl.BlockSpec(array.shape, lambda i: (0,) * array.ndim)

    args = [field, on, off, shifted, along_z, along_y]
    in_specs = [planes_spec(nx), planes_spec(width), planes_spec(width)]
    in_specs += [whole(shifted), whole(along_z), whole(along_y)]
    if stage == 2:
        args.append(orbitals)
        in_specs.append(planes_spec(nx))
    counts = [nx] + ([send, send] if send else [])
    result = pl.pallas_call(
        functools.partial(stage_body, stage, width, send),
        grid=(orbs // step,),
        in_specs=in_specs,
        out_specs=[planes_spec(count) for count in counts],
        out_shape=[jax.ShapeDtypeStruct((count, orbs, ny, nz), BF16) for count in counts],
        compiler_params=pltpu.CompilerParams(vmem_limit_bytes=32 * 1024 * 1024),
        cost_estimate=pl.CostEstimate(
            flops=orbs * nx * ny * nz * 1200, bytes_accessed=orbs * nx * ny * nz * 8, transcendentals=0
        ),
        name="stage%d" % stage,
    )(*args)
    return result


def prepare_body(core_ref, in_ref, all_ref, on_ref, off_ref):
    plane = pl.program_id(0)
    nx = pl.num_programs(0)
    block = in_ref[:, 0]
    all_ref[0] = block

    @pl.when(plane >= nx - REACH)
    def _():
        on_ref[0] = block

    @pl.when(plane < REACH)
    def _():
        off_ref[0] = block


def prepare(core, orbitals):
    orbs, nx, ny, nz = orbitals.shape
    out = (1, orbs, ny, nz)
    return pl.pallas_call(
        prepare_body,
        grid_spec=pltpu.PrefetchScalarGridSpec(
            num_scalar_prefetch=1,
            grid=(nx,),
            in_specs=[
                pl.BlockSpec(
                    (orbs, 1, ny, nz), lambda i, core: (0, i + core[0] * (nx - 1 - 2 * i), 0, 0)
                )
            ],
            out_specs=[
                pl.BlockSpec(out, lambda i, core: (i, 0, 0, 0)),
                pl.BlockSpec(out, lambda i, core: (jnp.maximum(i - (nx - REACH), 0), 0, 0, 0)),
                pl.BlockSpec(out, lambda i, core: (jnp.minimum(i, REACH - 1), 0, 0, 0)),
            ],
        ),
        out_shape=[
            jax.ShapeDtypeStruct((nx, orbs, ny, nz), BF16),
            jax.ShapeDtypeStruct((REACH, orbs, ny, nz), BF16),
            jax.ShapeDtypeStruct((REACH, orbs, ny, nz), BF16),
        ],
        compiler_params=pltpu.CompilerParams(vmem_limit_bytes=16 * 1024 * 1024),
        name="prepare",
    )(core, orbitals)


def exchange(on, off):
    count = lax.axis_size("domain")
    pairs = [(i, i ^ 1) for i in range(count)]
    facing = [(i, i + 1) for i in range(1, count - 1, 2)]
    facing += [(target, source) for source, target in facing]
    off = lax.ppermute(off, "domain", facing)
    on = lax.ppermute(on, "domain", pairs)
    return on, off


def rows_of(left, right):
    return lax.dot_general(
        left, right, (((1, 2), (1, 2)), ((), ())), preferred_element_type=F32
    )


def total_over_cells(partial):
    bands = lax.axis_size("band")
    what, rows, columns = partial.shape
    blocks = partial.reshape(what, bands, rows // bands, columns).swapaxes(0, 1)
    mine = lax.all_to_all(blocks, "band", 0, 0).sum(0)
    step = 1
    while step < lax.axis_size("domain"):
        mine = mine + lax.ppermute(
            mine, "domain", [(i, i ^ step) for i in range(lax.axis_size("domain"))]
        )
        step *= 2
    return mine


def per_device(orbitals, potential):
    count, nx, ny, nz = orbitals.shape
    bands = lax.axis_size("band")
    cells = float(nx * lax.axis_size("domain") * ny * nz)
    core = (lax.axis_index("domain") % 2).astype(jnp.int32)
    shifted = (potential - (1.5 * COEFS[0] + CENTER)) / HALF
    shifted = jnp.where(core == 0, shifted, shifted[::-1])
    along_z, along_y = stencil_matrices(ny, nz, 4)
    along_z, along_y = jnp.asarray(along_z), jnp.asarray(along_y)

    field, on, off = prepare(core.reshape(1), orbitals)
    on, off = exchange(on, off)
    first, on, off = run_stage(1, field, on, off, shifted, along_z, along_y)
    on, off = exchange(on, off)
    filtered, on, off = run_stage(2, first, on, off, shifted, along_z, along_y, field)
    on, off = exchange(on, off)
    all_f = lax.all_to_all(filtered, "band", 0, 0).reshape(bands * count, ny, nz)
    (applied,) = run_stage(3, filtered, on, off, shifted, along_z, along_y)
    all_a = lax.all_to_all(applied, "band", 0, 0).reshape(bands * count, ny, nz)
    corr = rows_of(all_f, all_f)
    proj = rows_of(all_a, all_f)
    proj = 0.5 * (proj + proj.T)
    totals = total_over_cells(jnp.stack([corr, proj])) / cells
    return (totals[0], totals[1])


def solution(mesh):
    return jax.shard_map(
        per_device,
        mesh=mesh,
        in_specs=(P("band", "domain", None, None), P("domain", None, None)),
        out_specs=(P("band", None), P("band", None)),
        check_vma=False,
    )
```

```python
import functools

import jax
import jax.numpy as jnp
import ml_dtypes
import numpy as np
from jax import lax
from jax.experimental import pallas as pl
from jax.experimental.pallas import tpu as pltpu
from jax.sharding import PartitionSpec as P

COEFS = (
    -5369.0 / 1800.0,
    12.0 / 7.0,
    -15.0 / 56.0,
    10.0 / 189.0,
    -1.0 / 112.0,
    2.0 / 1925.0,
    -1.0 / 16632.0,
)
CENTER = 8.0
HALF = 5.0
REACH = 6
OUTER = (1.0 / HALF, 2.0 / HALF, 1.0)
SHIFT = (-CENTER / HALF, -2.0 * CENTER / HALF, 0.0)
BF16 = jnp.bfloat16
F32 = jnp.float32
ORBS_STEP = 8
ROWS = 16
VMEM = 12 * 1024 * 1024
LINES = 64


def side_weights(stage):
    return [-0.5 * OUTER[stage - 1] * c for c in COEFS]


def band_matrix(stage, size):
    index = np.arange(size)
    gap = np.abs(index[:, None] - index[None, :])
    weights = np.array([0.0] + side_weights(stage)[1:])
    return np.where(gap <= REACH, weights[np.minimum(gap, REACH)], 0.0)


def split_two(matrix):
    high = matrix.astype(ml_dtypes.bfloat16)
    low = (matrix - high.astype(np.float64)).astype(ml_dtypes.bfloat16)
    return high, low


def stencil_matrices(stage, ny, nz, group):
    high, low = split_two(np.kron(np.eye(group), band_matrix(stage, ny)))
    along_y = np.concatenate([high, low], axis=1)
    along_z = np.concatenate(split_two(band_matrix(stage, nz)), axis=0)
    return jnp.asarray(along_y), jnp.asarray(along_z)


def stage_tables(stage, potential, core, group):
    ny, nz = potential.shape[1:]
    own = OUTER[stage - 1] * (potential - 1.5 * COEFS[0]) + SHIFT[stage - 1]
    own = jnp.where(core == 0, own, own[::-1])
    return (own, *stencil_matrices(stage, ny, nz, group))


def stage_body(stage, width, planes, unused, orbs, own, first, at, core_ref, *refs):
    c_ref, on_ref, off_ref, v_ref, my_ref, mz_ref = refs[:6]
    refs = refs[6:]
    if stage == 2:
        o_ref = refs[0]
        refs = refs[1:]
    outs = refs[unused:]
    core = core_ref[0]
    nx, ny, nz = v_ref.shape
    group = my_ref.shape[0] // ny

    def given(ref, b, p, rows):
        return ref[b, p + core * (nx - 1 - 2 * p), rows]

    def center(b, p, rows):
        return given(c_ref, first + b, p, rows) if stage == 1 else c_ref[p, own + b, rows]

    def beyond(b, i, rows):
        if stage == 1:
            return on_ref[b, i + core * (width - 1 - 2 * i), rows]
        return on_ref[width - 1 - i, b, rows]

    def before(b, i, rows):
        if stage == 1:
            return off_ref[b, (width - 1 - i) + core * (2 * i + 1 - width), rows]
        return off_ref[i, b, rows]

    everything = slice(0, ny)
    side = side_weights(stage)

    def orbital(b):
        lines = [center(b, p, everything) for p in range(nx)]
        sides = [jnp.concatenate(lines[q : q + group], axis=0) for q in range(0, nx, group)]
        part = jnp.concatenate(sides, axis=1)
        flat = jnp.concatenate(sides, axis=0)
        z_term = jnp.dot(
            jnp.concatenate([flat, flat], axis=1), mz_ref[...], preferred_element_type=F32
        ).reshape(nx, ny, nz)
        y_term = jnp.dot(
            my_ref[...], jnp.concatenate([part, part], axis=0), preferred_element_type=F32
        )
        y_parts = [
            y_term[:, k * nz : (k + 1) * nz].reshape(group, ny, nz) for k in range(nx // group)
        ]
        results = {}
        for r in range(0, ny, ROWS):
            rows = slice(r, r + ROWS)
            wide = {}
            for p in range(nx):
                wide[p] = center(b, p, rows).astype(F32)
            for i in range(width):
                wide[-1 - i] = before(b, i, rows).astype(F32)
                wide[nx + i] = beyond(b, i, rows).astype(F32)
            for p in range(nx):
                total = (
                    v_ref[p, rows] * wide[p]
                    + z_term[p, rows]
                    + y_parts[p // group][p % group, rows]
                )
                for s in range(1, REACH + 1):
                    near = []
                    twice = []
                    for q, gap in ((p - s, p), (p + s, nx - 1 - p)):
                        if q not in wide:
                            continue
                        outside = q < 0 or q >= nx
                        if outside and width < REACH and gap >= width:
                            twice.append(wide[q])
                        else:
                            near.append(wide[q])
                    if near:
                        total = total + side[s] * sum(near[1:], near[0])
                    if twice:
                        total = total + (2.0 * side[s]) * sum(twice[1:], twice[0])
                if stage == 2:
                    total = total - given(o_ref, first + b, p, rows).astype(F32)
                results[p, r] = total.astype(BF16)
        for (p, r), result in results.items():
            rows = slice(r, r + ROWS)
            outs[0][p, at + b, rows] = result
            if planes:
                if p >= nx - planes:
                    outs[1][p - (nx - planes), b, rows] = result
                if p < planes:
                    outs[2][p, b, rows] = result

    @pl.loop(0, orbs // ORBS_STEP)
    def _(i):
        for b in range(ORBS_STEP):
            orbital(i * ORBS_STEP + b)


def inside(array):
    return pltpu.with_memory_space_constraint(array, pltpu.VMEM)


def run_stage(stage, core, field, on, off, tables, chunk, orbs, orbitals=None, after=(), out=None, into=None):
    nx, ny, nz = tables[0].shape
    slots, at = out or (orbs, 0)
    width = REACH if stage < 3 else REACH // 2
    send = {1: REACH, 2: REACH // 2, 3: 0}[stage]
    first = chunk * orbs
    own = first if field.shape[1] > orbs else 0
    args = [field, on, off, *tables]
    if stage == 2:
        args.append(orbitals)
    args = [inside(array) for array in args]
    unused = list(after)
    aliases = {}
    if into is field:
        aliases = {1: 0}
    elif into is not None:
        aliases = {1 + len(args): 0}
        unused = [inside(into)] + unused
    out_shape = [pltpu.VMEM((nx, slots, ny, nz), BF16)]
    if send:
        out_shape += [pltpu.VMEM((send, orbs, ny, nz), BF16)] * 2
    vmem = pl.BlockSpec(memory_space=pltpu.VMEM)
    anywhere = pl.BlockSpec(memory_space=pl.ANY)
    held = 1 if aliases.get(1 + len(args)) == 0 else 0
    return pl.pallas_call(
        functools.partial(
            stage_body, stage, width, send, len(unused), orbs, own, first, at
        ),
        in_specs=[pl.BlockSpec(memory_space=pltpu.SMEM)]
        + [vmem] * (len(args) + held)
        + [anywhere] * (len(unused) - held),
        out_specs=[vmem] * len(out_shape),
        out_shape=out_shape,
        input_output_aliases=aliases,
        compiler_params=pltpu.CompilerParams(vmem_limit_bytes=VMEM),
        cost_estimate=pl.CostEstimate(
            flops=orbs * nx * ny * nz * 1200, bytes_accessed=orbs * nx * ny * nz * 8, transcendentals=0
        ),
        name="stage%d" % stage,
    )(core, *args, *unused)


def edges_body(first, far, core_ref, in_ref, on_ref, off_ref):
    core = core_ref[0]

    @pl.loop(0, on_ref.shape[0])
    def _(b):
        for i in range(REACH):
            on_ref[b, i] = in_ref[first + b, i + far * (1 - core)]
            off_ref[b, i] = in_ref[first + b, i + far * core]


def edges(core, orbitals, first, orbs):
    nx, ny, nz = orbitals.shape[1:]
    shape = pltpu.VMEM((orbs, REACH, ny, nz), BF16)
    vmem = pl.BlockSpec(memory_space=pltpu.VMEM)
    return pl.pallas_call(
        functools.partial(edges_body, first, nx - REACH),
        in_specs=[pl.BlockSpec(memory_space=pltpu.SMEM), vmem],
        out_specs=[vmem, vmem],
        out_shape=[shape, shape],
        compiler_params=pltpu.CompilerParams(vmem_limit_bytes=VMEM),
        name="edges",
    )(core, inside(orbitals))


def exchange(on, off):
    count = lax.axis_size("domain")
    pairs = [(i, i ^ 1) for i in range(count)]
    facing = [(i, i + 1) for i in range(1, count - 1, 2)]
    facing += [(target, source) for source, target in facing]
    on = lax.ppermute(on, "domain", pairs)
    off = lax.ppermute(off, "domain", facing)
    return on, off


def dot_rows(left, right):
    return lax.dot_general(left, right, (((1,), (1,)), ((), ())), preferred_element_type=F32)


def gram_body(scale, both_ref, out_ref):
    bands, orbs, ny, nz = both_ref.shape
    orbs //= 2
    count = bands * orbs

    def block(i, total):
        lines = pl.ds(pl.multiple_of(i * LINES, LINES), LINES)
        parts = [both_ref[:, :orbs, lines, :], both_ref[:, orbs:, lines, :]]
        f, a = [jnp.swapaxes(part.reshape(count, LINES, nz), 0, 1) for part in parts]
        for line in range(0, LINES, 2):
            right = jnp.concatenate([f[line], f[line + 1]], axis=1)
            left = jnp.concatenate([right, jnp.concatenate([a[line], a[line + 1]], axis=1)], axis=0)
            total = total + dot_rows(left, right)
        return total

    total = lax.fori_loop(0, ny // LINES, block, jnp.zeros((2 * count, count), F32))
    proj = total[count:]
    results = (total[:count] * scale, (0.5 * scale) * (proj + proj.T))
    for what in range(2):
        for band in range(bands):
            out_ref[band, what] = results[what][band * orbs : (band + 1) * orbs]


def gram(scale, both):
    bands, orbs, ny, nz = both.shape
    orbs //= 2
    vmem = pl.BlockSpec(memory_space=pltpu.VMEM)
    return pl.pallas_call(
        functools.partial(gram_body, scale),
        in_specs=[vmem],
        out_specs=vmem,
        out_shape=jax.ShapeDtypeStruct((bands, 2, orbs, bands * orbs), F32),
        compiler_params=pltpu.CompilerParams(vmem_limit_bytes=VMEM),
        name="gram",
    )(inside(both))


def swap(value, partner):
    pairs = []
    for b in range(8):
        for d in range(16):
            x, y, z, core = partner(b % 4, (b // 4) * 2 + d // 8, (d // 2) % 4, d % 2)
            pairs.append((b * 16 + d, ((y // 2) * 4 + x) * 16 + (y % 2) * 8 + z * 2 + core))
    return lax.ppermute(value, ("band", "domain"), pairs)


def total_over_cells(partial):
    domains = lax.axis_size("domain")
    half = domains // 2
    groups = [
        [band * domains + y * half + rest for band in range(8) for y in range(2)]
        for rest in range(half)
    ]
    pieces = jnp.broadcast_to(partial[:, None], (8, 2) + partial.shape[1:])
    pieces = pieces.reshape((16,) + partial.shape[1:])
    value = lax.all_to_all(pieces, ("band", "domain"), 0, 0, axis_index_groups=groups).sum(0)
    value = value + swap(value, lambda x, y, z, c: (x, y, z, 1 - c))
    value = value + swap(value, lambda x, y, z, c: (x, y, z ^ 1, c))
    value = value + swap(value, lambda x, y, z, c: (x, y, z ^ 3, c))
    return value


def per_device(orbitals, potential):
    count, nx, ny, nz = orbitals.shape
    cells = float(nx * lax.axis_size("domain") * ny * nz)
    core = (lax.axis_index("domain") % 2).astype(jnp.int32)
    tables = [stage_tables(stage, potential, core, nx // 2) for stage in (1, 2, 3)]
    half = count // 2
    core = core.reshape(1)
    room = 2 * count

    halos = [edges(core, orbitals, c * half, half) for c in range(2)]
    later = halos[1][1]
    halos = [exchange(*halo) for halo in halos]
    first0, on, off = run_stage(1, core, orbitals, *halos[0], tables[0], 0, half, after=(later,))
    halos[0] = exchange(on, off)
    first1, on, later = run_stage(1, core, orbitals, *halos[1], tables[0], 1, half)
    halos[1] = exchange(on, later)
    both, on, off = run_stage(
        2, core, first0, *halos[0], tables[1], 0, half, orbitals, after=(later,), out=(room, 0)
    )
    halos[0] = exchange(on, off)
    both, on, off = run_stage(
        2, core, first1, *halos[1], tables[1], 1, half, orbitals, out=(room, half), into=both
    )
    halos[1] = exchange(on, off)
    for c in range(2):
        (both,) = run_stage(
            3, core, both, *halos[c], tables[2], c, half, out=(room, count + c * half), into=both
        )
    both = lax.all_to_all(both, "band", 0, 0)
    totals = total_over_cells(gram(1.0 / cells, both))
    return (totals[0], totals[1])


def solution(mesh):
    return jax.shard_map(
        per_device,
        mesh=mesh,
        in_specs=(P("band", "domain", None, None), P("domain", None, None)),
        out_specs=(P("band", None), P("band", None)),
        check_vma=False,
    )
```

```python
import functools

import jax
import jax.numpy as jnp
import ml_dtypes
import numpy as np
from jax import lax
from jax.experimental import pallas as pl
from jax.experimental.pallas import tpu as pltpu
from jax.sharding import PartitionSpec as P

COEFS = (
    -5369.0 / 1800.0,
    12.0 / 7.0,
    -15.0 / 56.0,
    10.0 / 189.0,
    -1.0 / 112.0,
    2.0 / 1925.0,
    -1.0 / 16632.0,
)
CENTER = 8.0
HALF = 5.0
REACH = 6
OUTER = (1.0 / HALF, 2.0 / HALF, 1.0)
SHIFT = (-CENTER / HALF, -2.0 * CENTER / HALF, 0.0)
BF16 = jnp.bfloat16
F32 = jnp.float32
ORBS_STEP = 8
ROWS = 16
VMEM = 12 * 1024 * 1024
LINES = 64


def side_weights(stage):
    return [-0.5 * OUTER[stage - 1] * c for c in COEFS]


def band_matrix(stage, size):
    index = np.arange(size)
    gap = np.abs(index[:, None] - index[None, :])
    weights = np.array([0.0] + side_weights(stage)[1:])
    return np.where(gap <= REACH, weights[np.minimum(gap, REACH)], 0.0)


def split_two(matrix):
    high = matrix.astype(ml_dtypes.bfloat16)
    low = (matrix - high.astype(np.float64)).astype(ml_dtypes.bfloat16)
    return high, low


def stencil_matrices(stage, ny, nz, group):
    high, low = split_two(np.kron(np.eye(group), band_matrix(stage, ny)))
    along_y = np.concatenate([high, low], axis=1)
    along_z = np.concatenate(split_two(band_matrix(stage, nz)), axis=0)
    return jnp.asarray(along_y), jnp.asarray(along_z)


def stage_tables(stage, potential, core, group):
    ny, nz = potential.shape[1:]
    own = OUTER[stage - 1] * (potential - 1.5 * COEFS[0]) + SHIFT[stage - 1]
    own = jnp.where(core == 0, own, own[::-1])
    return (own, *stencil_matrices(stage, ny, nz, group))


def stage_body(stage, width, planes, unused, orbs, own, first, at, core_ref, *refs):
    c_ref, off_ref, on_ref, v_ref, my_ref, mz_ref = refs[:6]
    refs = refs[6:]
    if stage == 2:
        o_ref = refs[0]
        refs = refs[1:]
    outs = refs[unused:]
    core = core_ref[0]
    nx, ny, nz = v_ref.shape
    group = my_ref.shape[0] // ny

    def given(ref, b, p, rows):
        return ref[b, p + core * (nx - 1 - 2 * p), rows]

    def center(b, p, rows):
        return given(c_ref, first + b, p, rows) if stage == 1 else c_ref[p, own + b, rows]

    def beyond(b, i, rows):
        if stage == 1:
            return on_ref[b, i + core * (width - 1 - 2 * i), rows]
        return on_ref[width - 1 - i, b, rows]

    def before(b, i, rows):
        if stage == 1:
            return off_ref[b, (width - 1 - i) + core * (2 * i + 1 - width), rows]
        return off_ref[i, b, rows]

    everything = slice(0, ny)
    side = side_weights(stage)

    def orbital(b):
        lines = [center(b, p, everything) for p in range(nx)]
        sides = [jnp.concatenate(lines[q : q + group], axis=0) for q in range(0, nx, group)]
        part = jnp.concatenate(sides, axis=1)
        flat = jnp.concatenate(sides, axis=0)
        z_term = jnp.dot(
            jnp.concatenate([flat, flat], axis=1), mz_ref[...], preferred_element_type=F32
        ).reshape(nx, ny, nz)
        y_term = jnp.dot(
            my_ref[...], jnp.concatenate([part, part], axis=0), preferred_element_type=F32
        )
        y_parts = [
            y_term[:, k * nz : (k + 1) * nz].reshape(group, ny, nz) for k in range(nx // group)
        ]
        results = {}
        for r in range(0, ny, ROWS):
            rows = slice(r, r + ROWS)
            wide = {}
            for p in range(nx):
                wide[p] = center(b, p, rows).astype(F32)
            for i in range(width):
                wide[-1 - i] = before(b, i, rows).astype(F32)
                wide[nx + i] = beyond(b, i, rows).astype(F32)
            for p in range(nx):
                total = (
                    v_ref[p, rows] * wide[p]
                    + z_term[p, rows]
                    + y_parts[p // group][p % group, rows]
                )
                for s in range(1, REACH + 1):
                    near = []
                    twice = []
                    for q, gap in ((p - s, p), (p + s, nx - 1 - p)):
                        if q not in wide:
                            continue
                        outside = q < 0 or q >= nx
                        if outside and width < REACH and gap >= width:
                            twice.append(wide[q])
                        else:
                            near.append(wide[q])
                    if near:
                        total = total + side[s] * sum(near[1:], near[0])
                    if twice:
                        total = total + (2.0 * side[s]) * sum(twice[1:], twice[0])
                if stage == 2:
                    total = total - given(o_ref, first + b, p, rows).astype(F32)
                results[p, r] = total.astype(BF16)
        for (p, r), result in results.items():
            rows = slice(r, r + ROWS)
            outs[0][p, at + b, rows] = result
            if planes:
                if p >= nx - planes:
                    outs[1][p - (nx - planes), b, rows] = result
                if p < planes:
                    outs[2][p, b, rows] = result

    @pl.loop(0, orbs // ORBS_STEP)
    def _(i):
        for b in range(ORBS_STEP):
            orbital(i * ORBS_STEP + b)


def inside(array):
    return pltpu.with_memory_space_constraint(array, pltpu.VMEM)


def run_stage(stage, core, field, on, off, tables, chunk, orbs, orbitals=None, after=(), out=None, into=None):
    nx, ny, nz = tables[0].shape
    slots, at = out or (orbs, 0)
    width = REACH if stage < 3 else REACH // 2
    send = {1: REACH, 2: REACH // 2, 3: 0}[stage]
    first = chunk * orbs
    own = first if field.shape[1] > orbs else 0
    args = [field, off, on, *tables]
    if stage == 2:
        args.append(orbitals)
    args = [inside(array) for array in args]
    unused = list(after)
    aliases = {}
    if into is field:
        aliases = {1: 0}
    elif into is not None:
        aliases = {1 + len(args): 0}
        unused = [inside(into)] + unused
    out_shape = [pltpu.VMEM((nx, slots, ny, nz), BF16)]
    if send:
        out_shape += [pltpu.VMEM((send, orbs, ny, nz), BF16)] * 2
    vmem = pl.BlockSpec(memory_space=pltpu.VMEM)
    anywhere = pl.BlockSpec(memory_space=pl.ANY)
    held = 1 if aliases.get(1 + len(args)) == 0 else 0
    return pl.pallas_call(
        functools.partial(
            stage_body, stage, width, send, len(unused), orbs, own, first, at
        ),
        in_specs=[pl.BlockSpec(memory_space=pltpu.SMEM)]
        + [vmem] * (len(args) + held)
        + [anywhere] * (len(unused) - held),
        out_specs=[vmem] * len(out_shape),
        out_shape=out_shape,
        input_output_aliases=aliases,
        compiler_params=pltpu.CompilerParams(vmem_limit_bytes=VMEM),
        cost_estimate=pl.CostEstimate(
            flops=orbs * nx * ny * nz * 1200, bytes_accessed=orbs * nx * ny * nz * 8, transcendentals=0
        ),
        name="stage%d" % stage,
    )(core, *args, *unused)


def edges_body(first, far, core_ref, in_ref, on_ref, off_ref):
    core = core_ref[0]
    for b in range(on_ref.shape[0]):
        on = [in_ref[first + b, i + far * (1 - core)] for i in range(REACH)]
        off = [in_ref[first + b, i + far * core] for i in range(REACH)]
        for i in range(REACH):
            on_ref[b, i] = on[i]
            off_ref[b, i] = off[i]


def edges(core, orbitals, first, orbs):
    nx, ny, nz = orbitals.shape[1:]
    shape = pltpu.VMEM((orbs, REACH, ny, nz), BF16)
    vmem = pl.BlockSpec(memory_space=pltpu.VMEM)
    return pl.pallas_call(
        functools.partial(edges_body, first, nx - REACH),
        in_specs=[pl.BlockSpec(memory_space=pltpu.SMEM), vmem],
        out_specs=[vmem, vmem],
        out_shape=[shape, shape],
        compiler_params=pltpu.CompilerParams(vmem_limit_bytes=VMEM),
        name="edges",
    )(core, inside(orbitals))


def exchange(on, off):
    count = lax.axis_size("domain")
    pairs = [(i, i ^ 1) for i in range(count)]
    facing = [(i, i + 1) for i in range(1, count - 1, 2)]
    facing += [(target, source) for source, target in facing]
    on = lax.ppermute(on, "domain", pairs)
    off = lax.ppermute(off, "domain", facing)
    return on, off


def dot_rows(left, right):
    return lax.dot_general(left, right, (((1,), (1,)), ((), ())), preferred_element_type=F32)


def gram_body(scale, both_ref, out_ref):
    bands, orbs, ny, nz = both_ref.shape
    orbs //= 2
    count = bands * orbs

    def block(i, total):
        lines = pl.ds(pl.multiple_of(i * LINES, LINES), LINES)
        parts = [both_ref[:, :orbs, lines, :], both_ref[:, orbs:, lines, :]]
        f, a = [jnp.swapaxes(part.reshape(count, LINES, nz), 0, 1) for part in parts]
        for line in range(0, LINES, 2):
            right = jnp.concatenate([f[line], f[line + 1]], axis=1)
            left = jnp.concatenate([right, jnp.concatenate([a[line], a[line + 1]], axis=1)], axis=0)
            total = total + dot_rows(left, right)
        return total

    total = lax.fori_loop(0, ny // LINES, block, jnp.zeros((2 * count, count), F32))
    proj = total[count:]
    results = (total[:count] * scale, (0.5 * scale) * (proj + proj.T))
    for what in range(2):
        for band in range(bands):
            out_ref[band, what] = results[what][band * orbs : (band + 1) * orbs]


def gram(scale, both):
    bands, orbs, ny, nz = both.shape
    orbs //= 2
    vmem = pl.BlockSpec(memory_space=pltpu.VMEM)
    return pl.pallas_call(
        functools.partial(gram_body, scale),
        in_specs=[vmem],
        out_specs=vmem,
        out_shape=jax.ShapeDtypeStruct((bands, 2, orbs, bands * orbs), F32),
        compiler_params=pltpu.CompilerParams(vmem_limit_bytes=VMEM),
        name="gram",
    )(inside(both))


def swap(value, partner):
    pairs = []
    for b in range(8):
        for d in range(16):
            x, y, z, core = partner(b % 4, (b // 4) * 2 + d // 8, (d // 2) % 4, d % 2)
            pairs.append((b * 16 + d, ((y // 2) * 4 + x) * 16 + (y % 2) * 8 + z * 2 + core))
    return lax.ppermute(value, ("band", "domain"), pairs)


def total_over_cells(partial):
    domains = lax.axis_size("domain")
    half = domains // 2
    groups = [
        [band * domains + y * half + rest for band in range(8) for y in range(2)]
        for rest in range(half)
    ]
    pieces = jnp.broadcast_to(partial[:, None], (8, 2) + partial.shape[1:])
    pieces = pieces.reshape((16,) + partial.shape[1:])
    value = lax.all_to_all(pieces, ("band", "domain"), 0, 0, axis_index_groups=groups).sum(0)
    value = value + swap(value, lambda x, y, z, c: (x, y, z, 1 - c))
    value = value + swap(value, lambda x, y, z, c: (x, y, z ^ 1, c))
    value = value + swap(value, lambda x, y, z, c: (x, y, z ^ 3, c))
    return value


def per_device(orbitals, potential):
    count, nx, ny, nz = orbitals.shape
    cells = float(nx * lax.axis_size("domain") * ny * nz)
    core = (lax.axis_index("domain") % 2).astype(jnp.int32)
    tables = [stage_tables(stage, potential, core, nx // 2) for stage in (1, 2, 3)]
    half = count // 2
    core = core.reshape(1)
    room = 2 * count

    halos = [edges(core, orbitals, c * half, half) for c in range(2)]
    later = halos[1][1]
    halos = [exchange(*halo) for halo in halos]
    first0, on, off = run_stage(1, core, orbitals, *halos[0], tables[0], 0, half, after=(later,))
    halos[0] = exchange(on, off)
    first1, on, later = run_stage(1, core, orbitals, *halos[1], tables[0], 1, half)
    halos[1] = exchange(on, later)
    both, on, off = run_stage(
        2, core, first0, *halos[0], tables[1], 0, half, orbitals, after=(later,), out=(room, 0)
    )
    halos[0] = exchange(on, off)
    both, on, off = run_stage(
        2, core, first1, *halos[1], tables[1], 1, half, orbitals, out=(room, half), into=both
    )
    halos[1] = exchange(on, off)
    for c in range(2):
        (both,) = run_stage(
            3, core, both, *halos[c], tables[2], c, half, out=(room, count + c * half), into=both
        )
    both = lax.all_to_all(both, "band", 0, 0)
    totals = total_over_cells(gram(1.0 / cells, both))
    return (totals[0], totals[1])


def solution(mesh):
    return jax.shard_map(
        per_device,
        mesh=mesh,
        in_specs=(P("band", "domain", None, None), P("domain", None, None)),
        out_specs=(P("band", None), P("band", None)),
        check_vma=False,
    )
```

```python
import functools

import jax
import jax.numpy as jnp
import ml_dtypes
import numpy as np
from jax import lax
from jax.experimental import pallas as pl
from jax.experimental.pallas import tpu as pltpu
from jax.sharding import PartitionSpec as P

COEFS = (
    -5369.0 / 1800.0,
    12.0 / 7.0,
    -15.0 / 56.0,
    10.0 / 189.0,
    -1.0 / 112.0,
    2.0 / 1925.0,
    -1.0 / 16632.0,
)
CENTER = 8.0
HALF = 5.0
REACH = 6
OUTER = (1.0 / HALF, 2.0 / HALF, 1.0)
SHIFT = (-CENTER / HALF, -2.0 * CENTER / HALF, 0.0)
BF16 = jnp.bfloat16
F32 = jnp.float32
ZROWS = 16
NARROW = REACH // 2
ROWS = 16
VMEM = 12 * 1024 * 1024


def side_weights(stage):
    return [-0.5 * OUTER[stage - 1] * c for c in COEFS]


def band_matrix(stage, size):
    index = np.arange(size)
    gap = np.abs(index[:, None] - index[None, :])
    weights = np.array([0.0] + side_weights(stage)[1:])
    return np.where(gap <= REACH, weights[np.minimum(gap, REACH)], 0.0)


def split_two(matrix):
    high = matrix.astype(ml_dtypes.bfloat16)
    low = (matrix - high.astype(np.float64)).astype(ml_dtypes.bfloat16)
    return high, low


def stencil_matrices(stage, ny, nz, group):
    high, low = split_two(np.kron(np.eye(group), band_matrix(stage, ny)))
    along_y = np.concatenate([high, low], axis=1)
    along_z = np.concatenate(split_two(band_matrix(stage, nz)), axis=0)
    return jnp.asarray(along_y), jnp.asarray(along_z)


def stage_tables(stage, potential, core, group):
    ny, nz = potential.shape[1:]
    own = OUTER[stage - 1] * (potential - 1.5 * COEFS[0]) + SHIFT[stage - 1]
    own = jnp.where(core == 0, own, own[::-1])
    return (own, *stencil_matrices(stage, ny, nz, group))


def stage_body(stage, unused, orbs, first, at, core_ref, *refs):
    width = REACH
    c_ref, off_ref, on_ref, v_ref, my_ref, mz_ref = refs[:6]
    refs = refs[6:]
    if stage == 2:
        o_ref = refs[0]
        refs = refs[1:]
    outs = refs[unused:]
    core = core_ref[0]
    nx, ny, nz = v_ref.shape
    group = my_ref.shape[0] // ny

    def given(ref, b, p, rows):
        return ref[b, p + core * (nx - 1 - 2 * p), rows]

    def center(b, p, rows):
        return given(c_ref, first + b, p, rows) if stage == 1 else c_ref[p, b, rows]

    def beyond(b, i, rows):
        if stage == 1:
            return on_ref[b, i + core * (width - 1 - 2 * i), rows]
        return on_ref[width - 1 - i, b, rows]

    def before(b, i, rows):
        if stage == 1:
            return off_ref[b, (width - 1 - i) + core * (2 * i + 1 - width), rows]
        return off_ref[i, b, rows]

    everything = slice(0, ny)
    side = side_weights(stage)

    def orbital(b):
        lines = [center(b, p, everything) for p in range(nx)]
        sides = [jnp.concatenate(lines[q : q + group], axis=0) for q in range(0, nx, group)]
        part = jnp.concatenate(sides, axis=1)
        flat = jnp.concatenate(sides, axis=0)
        z_term = jnp.dot(
            jnp.concatenate([flat, flat], axis=1), mz_ref[...], preferred_element_type=F32
        ).reshape(nx, ny, nz)
        y_term = jnp.dot(
            my_ref[...], jnp.concatenate([part, part], axis=0), preferred_element_type=F32
        )
        y_parts = [
            y_term[:, k * nz : (k + 1) * nz].reshape(group, ny, nz) for k in range(nx // group)
        ]
        results = {}
        for r in range(0, ny, ROWS):
            rows = slice(r, r + ROWS)
            wide = {}
            for p in range(nx):
                wide[p] = center(b, p, rows).astype(F32)
            for i in range(width):
                wide[-1 - i] = before(b, i, rows).astype(F32)
                wide[nx + i] = beyond(b, i, rows).astype(F32)
            for p in range(nx):
                total = (
                    v_ref[p, rows] * wide[p]
                    + z_term[p, rows]
                    + y_parts[p // group][p % group, rows]
                )
                for s in range(1, REACH + 1):
                    near = []
                    for q in (p - s, p + s):
                        near.append(wide[q])
                    total = total + side[s] * sum(near[1:], near[0])
                if stage == 2:
                    total = total - given(o_ref, first + b, p, rows).astype(F32)
                results[p, r] = total.astype(BF16)
        return results

    if stage == 1:
        for b in range(orbs):
            for (p, r), result in orbital(b).items():
                rows = slice(r, r + ROWS)
                outs[0][p, b, rows] = result
                if p >= nx - REACH:
                    outs[1][p - (nx - REACH), b, rows] = result
                if p < REACH:
                    outs[2][p, b, rows] = result
    else:
        unit = (iota2(nz, 0) == iota2(nz, 1)).astype(F32).astype(BF16)
        for b in range(orbs // 2):
            pair = [orbital(b), orbital(b + orbs // 2)]
            for p in range(nx):
                both = jnp.concatenate(
                    [one[p, r] for one in pair for r in range(0, ny, ROWS)], axis=0
                )
                turned = both.T
                for block in range(nz // ZROWS):
                    outs[0][block, p, at + b] = turned[block * ZROWS : (block + 1) * ZROWS]


def iota2(size, dim):
    return lax.broadcasted_iota(jnp.int32, (size, size), dim)


def dot_rows(left, right):
    return lax.dot_general(left, right, (((1,), (1,)), ((), ())), preferred_element_type=F32)


def inside(array):
    return pltpu.with_memory_space_constraint(array, pltpu.VMEM)


def run_stage(stage, core, field, on, off, tables, first, orbs, orbitals=None, after=(), into=None):
    nx, ny, nz = tables[0].shape
    args = [field, off, on, *tables]
    if stage == 2:
        args.append(orbitals)
        count = orbitals.shape[0]
        out_shape = [pltpu.VMEM((nz // ZROWS, nx, count // 2, ZROWS, 2 * ny), BF16)]
    else:
        out_shape = [pltpu.VMEM((n, orbs, ny, nz), BF16) for n in (nx, REACH, REACH)]
    args = [inside(array) for array in args]
    unused = list(after)
    aliases = {}
    vmem = pl.BlockSpec(memory_space=pltpu.VMEM)
    specs = [vmem] * len(args) + [pl.BlockSpec(memory_space=pl.ANY)] * len(unused)
    if into is not None:
        aliases = {1 + len(args): 0}
        unused = [inside(into)] + unused
        specs.insert(len(args), vmem)
    return pl.pallas_call(
        functools.partial(stage_body, stage, len(unused), orbs, first, first // 2),
        in_specs=[pl.BlockSpec(memory_space=pltpu.SMEM)] + specs,
        out_specs=[vmem] * len(out_shape),
        out_shape=out_shape,
        input_output_aliases=aliases,
        compiler_params=pltpu.CompilerParams(vmem_limit_bytes=VMEM),
        cost_estimate=pl.CostEstimate(
            flops=orbs * nx * ny * nz * 1200, bytes_accessed=orbs * nx * ny * nz * 8, transcendentals=0
        ),
        name="stage%d" % stage,
    )(core, *args, *unused)


def edges_body(first, far, core_ref, in_ref, on_ref, off_ref):
    core = core_ref[0]
    for b in range(on_ref.shape[0]):
        on = [in_ref[first + b, i + far * (1 - core)] for i in range(REACH)]
        off = [in_ref[first + b, i + far * core] for i in range(REACH)]
        for i in range(REACH):
            on_ref[b, i] = on[i]
            off_ref[b, i] = off[i]


def edges(core, orbitals, first, orbs):
    nx, ny, nz = orbitals.shape[1:]
    shape = pltpu.VMEM((orbs, REACH, ny, nz), BF16)
    vmem = pl.BlockSpec(memory_space=pltpu.VMEM)
    return pl.pallas_call(
        functools.partial(edges_body, first, nx - REACH),
        in_specs=[pl.BlockSpec(memory_space=pltpu.SMEM), vmem],
        out_specs=[vmem, vmem],
        out_shape=[shape, shape],
        compiler_params=pltpu.CompilerParams(vmem_limit_bytes=VMEM),
        name="edges",
    )(core, inside(orbitals))


def exchange(on, off):
    count = lax.axis_size("domain")
    pairs = [(i, i ^ 1) for i in range(count)]
    facing = [(i, i + 1) for i in range(1, count - 1, 2)]
    facing += [(target, source) for source, target in facing]
    on = lax.ppermute(on, "domain", pairs)
    off = lax.ppermute(off, "domain", facing)
    return on, off


def turn_body(place_ref, v_ref, out_ref, held_ref):
    band, core = place_ref[0], place_ref[1]
    nx = v_ref.shape[0]
    for p in range(nx):
        line = v_ref[p + core * (nx - 1 - 2 * p)] - 1.5 * COEFS[0]
        held_ref[p] = jnp.concatenate([line, line], axis=0).T
    for p in range(nx):
        out_ref[p] = held_ref[p, pl.ds(pl.multiple_of(band * ZROWS, ZROWS), ZROWS), :]


def turn(band, core, potential):
    nx, ny, nz = potential.shape
    vmem = pl.BlockSpec(memory_space=pltpu.VMEM)
    return pl.pallas_call(
        turn_body,
        in_specs=[pl.BlockSpec(memory_space=pltpu.SMEM), vmem],
        out_specs=vmem,
        out_shape=pltpu.VMEM((nx, ZROWS, 2 * ny), F32),
        scratch_shapes=[pltpu.VMEM((nx, nz, 2 * ny), F32)],
        compiler_params=pltpu.CompilerParams(vmem_limit_bytes=VMEM),
        name="turn",
    )(jnp.stack([band, core]).astype(jnp.int32), inside(potential))


def block_matrices(nz_block, ny, blocks):
    side = side_weights(3)
    reach = NARROW
    low, high = np.zeros((nz_block, reach)), np.zeros((nz_block, reach))
    for i in range(nz_block):
        for j in range(reach):
            gap = i + reach - j
            if gap <= REACH:
                low[i, j] = side[gap] * (1 if i < reach else 2)
            gap = nz_block - i + j
            if gap <= REACH:
                high[i, j] = side[gap] * (1 if nz_block - 1 - i < reach else 2)
    unit = np.eye(blocks)
    own = split_two(np.kron(unit, band_matrix(3, nz_block)))
    beside = split_two(np.concatenate([np.kron(unit, low), np.kron(unit, high)], axis=1))
    along_z, beside = np.concatenate(own, axis=1), np.concatenate(beside, axis=1)
    twice = np.kron(np.eye(2), band_matrix(3, ny))
    along_y = np.concatenate(split_two(twice), axis=0)
    pick = np.zeros((2, reach, nz_block))
    for j in range(reach):
        pick[0, j, j] = 1
        pick[1, j, nz_block - reach + j] = 1
    pick = np.concatenate([np.kron(unit, pick[0]), np.kron(unit, pick[1])], axis=0)
    return along_z, along_y, beside, pick.astype(ml_dtypes.bfloat16)


def two_planes(ref, s, p):
    pairs, rows, lanes = ref.shape[2:]
    return jnp.concatenate([ref[s, p + i].reshape(pairs * rows, lanes) for i in range(2)], axis=0)


def borders_body(f_ref, pick_ref, on_ref, off_ref, low_ref, high_ref):
    bands, nx = f_ref.shape[:2]
    count = low_ref.shape[2]
    for s in range(bands):
        for p in range(0, nx, 2):
            rows = jnp.dot(pick_ref[...], two_planes(f_ref, s, p), preferred_element_type=F32)
            rows = rows.astype(BF16)
            low_ref[s, p // 2] = rows[:count]
            high_ref[s, p // 2] = rows[count:]
        for p in range(NARROW):
            off_ref[s, p] = f_ref[s, p]
            on_ref[s, p] = f_ref[s, nx - NARROW + p]


def borders(filtered, pick):
    bands, nx, pairs, rows, lanes = filtered.shape
    vmem = pl.BlockSpec(memory_space=pltpu.VMEM)
    planes = pltpu.VMEM((bands, NARROW, pairs, rows, lanes), BF16)
    lines = pltpu.VMEM((bands, nx // 2, pick.shape[0] // 2, lanes), BF16)
    return pl.pallas_call(
        borders_body,
        in_specs=[vmem, vmem],
        out_specs=[vmem] * 4,
        out_shape=[planes, planes, lines, lines],
        compiler_params=pltpu.CompilerParams(vmem_limit_bytes=VMEM),
        name="borders",
    )(filtered, inside(pick))


def local_body(f_ref, v_ref, mz_ref, my_ref, out_ref):
    bands, nx, pairs, rows, lanes = f_ref.shape
    side = side_weights(3)
    for s in range(bands):
        z_terms, y_terms = [], []
        for p in range(0, nx, 4):
            data = jnp.concatenate([two_planes(f_ref, s, p + i) for i in (0, 2)], axis=1)
            term = jnp.dot(
                mz_ref[...], jnp.concatenate([data, data], axis=0), preferred_element_type=F32
            )
            for i in range(2):
                half = term[:, i * lanes : (i + 1) * lanes].reshape(2, pairs, rows, lanes)
                z_terms += [half[0], half[1]]
        for p in range(0, nx, 2):
            data = two_planes(f_ref, s, p)
            term = jnp.dot(
                jnp.concatenate([data, data], axis=1), my_ref[...], preferred_element_type=F32
            ).reshape(2, pairs, rows, lanes)
            y_terms += [term[0], term[1]]
        results = {}
        for q in range(pairs):
            wide = [f_ref[s, p, q].astype(F32) for p in range(nx)]
            for p in range(nx):
                total = v_ref[p] * wide[p] + z_terms[p][q] + y_terms[p][q]
                for gap in range(1, REACH + 1):
                    near = [wide[other] for other in (p - gap, p + gap) if 0 <= other < nx]
                    if near:
                        total = total + side[gap] * sum(near[1:], near[0])
                results[p, q] = total.astype(BF16)
        for (p, q), result in results.items():
            out_ref[s, p, q] = result


def local_stage(filtered, own, along_z, along_y):
    vmem = pl.BlockSpec(memory_space=pltpu.VMEM)
    args = [inside(array) for array in (filtered, own, along_z, along_y)]
    return pl.pallas_call(
        local_body,
        in_specs=[vmem] * len(args),
        out_specs=vmem,
        out_shape=pltpu.VMEM(filtered.shape, BF16),
        compiler_params=pltpu.CompilerParams(vmem_limit_bytes=VMEM),
        cost_estimate=pl.CostEstimate(flops=10**9, bytes_accessed=2**22, transcendentals=0),
        name="local",
    )(*args)


def orbital_rows(block):
    count, rows, lanes = block.shape
    half = lanes // 2
    change = iota2(lanes, 0) == (iota2(lanes, 1) + half) % lanes
    change = change.astype(F32).astype(BF16)
    block = jnp.swapaxes(block, 0, 1)
    changed = jnp.dot(block.reshape(rows * count, lanes), change, preferred_element_type=F32)
    changed = changed.astype(BF16).reshape(rows, count, lanes)
    first = lax.broadcasted_iota(jnp.int32, (count, lanes), 1) < half
    parts = []
    for z in range(0, rows, 2):
        even = jnp.where(first, block[z], changed[z + 1])
        odd = jnp.where(first, changed[z], block[z + 1])
        parts.append(jnp.concatenate([even, odd], axis=0))
    return [jnp.concatenate(parts[i : i + 2], axis=1) for i in range(0, len(parts), 2)]


def natural_rows(square, pairs):
    size = square.shape[0]
    four = pairs // 2
    parts = []
    for row in range(0, size, four):
        band, chunk, half = row // (4 * four), (row // (2 * four)) % 2, (row // four) % 2
        start = half * (size // 2) + band * pairs + chunk * four
        parts.append(square[start : start + four])
    return jnp.concatenate(parts, axis=0)


def gram_body(scale, f_ref, a_ref, corr_ref, total_ref, right_ref):
    bands, nx, pairs, rows, lanes = f_ref.shape
    count = bands * pairs

    def block(p, total):
        right = orbital_rows(f_ref[:, p].reshape(count, rows, lanes))
        left = orbital_rows(a_ref[:, p].reshape(count, rows, lanes))
        for i, (one, other) in enumerate(zip(right, left)):
            right_ref[p, i] = one
            total = total + dot_rows(jnp.concatenate([one, other], axis=0), one)
        return total

    total = lax.fori_loop(0, nx, block, jnp.zeros((4 * count, 2 * count), F32))
    total_ref[...] = total[2 * count :]
    corr = natural_rows(total[: 2 * count] * scale, pairs).T
    corr_ref[...] = natural_rows(corr, pairs)


def gram(scale, filtered, applied):
    bands, nx, pairs, rows, lanes = filtered.shape
    size = 2 * bands * pairs
    vmem = pl.BlockSpec(memory_space=pltpu.VMEM)
    return pl.pallas_call(
        functools.partial(gram_body, scale),
        in_specs=[vmem, vmem],
        out_specs=[vmem] * 3,
        out_shape=[
            pltpu.VMEM((size, size), F32),
            pltpu.VMEM((size, size), F32),
            pltpu.VMEM((nx, rows // 4, size, 2 * lanes), BF16),
        ],
        compiler_params=pltpu.CompilerParams(vmem_limit_bytes=VMEM),
        cost_estimate=pl.CostEstimate(flops=10**9, bytes_accessed=2**22, transcendentals=0),
        name="gram",
    )(inside(filtered), inside(applied))


def finish_body(
    scale,
    low_ref,
    high_ref,
    off_ref,
    on_ref,
    beside_ref,
    corr_ref,
    total_ref,
    right_ref,
    out_ref,
    cross_ref,
):
    bands, width, pairs, rows, lanes = off_ref.shape
    nx = right_ref.shape[0]
    count = bands * pairs
    side = side_weights(3)
    for s in range(bands):
        z_terms = []
        for p in range(0, nx, 4):
            halo = jnp.concatenate(
                [
                    jnp.concatenate([low_ref[s, p // 2 + i], high_ref[s, p // 2 + i]], axis=0)
                    for i in range(2)
                ],
                axis=1,
            )
            term = jnp.dot(
                beside_ref[...],
                jnp.concatenate([halo, halo], axis=0),
                preferred_element_type=F32,
            )
            for i in range(2):
                half = term[:, i * lanes : (i + 1) * lanes].reshape(2, pairs, rows, lanes)
                z_terms += [half[0], half[1]]
        for q in range(pairs):
            off = [off_ref[s, i, q].astype(F32) for i in range(width)]
            on = [on_ref[s, width - 1 - i, q].astype(F32) for i in range(width)]
            for p in range(nx):
                total = z_terms[p][q]
                for beyond, depth in ((off, p), (on, nx - 1 - p)):
                    weight = 2.0 if depth >= width else 1.0
                    for i in range(width):
                        if depth + i + 1 <= REACH:
                            total = total + (weight * side[depth + i + 1]) * beyond[i]
                cross_ref[s, p, q] = total.astype(BF16)

    def block(p, total):
        left = orbital_rows(cross_ref[:, p].reshape(count, rows, lanes))
        for i, one in enumerate(left):
            total = total + dot_rows(one, right_ref[p, i])
        return total

    proj = lax.fori_loop(0, nx, block, total_ref[...])
    proj = natural_rows((0.5 * scale) * (proj + proj.T), pairs).T
    proj = natural_rows(proj, pairs)
    size = 2 * pairs
    for band in range(bands):
        out_ref[band, 0] = corr_ref[band * size : (band + 1) * size]
        out_ref[band, 1] = proj[band * size : (band + 1) * size]


def finish(scale, halos, beside, corr, total, right):
    bands, _, pairs, rows, lanes = halos[2].shape
    vmem = pl.BlockSpec(memory_space=pltpu.VMEM)
    args = [inside(array) for array in (*halos, beside, corr, total, right)]
    return pl.pallas_call(
        functools.partial(finish_body, scale),
        in_specs=[vmem] * len(args),
        out_specs=vmem,
        out_shape=jax.ShapeDtypeStruct((bands, 2, 2 * pairs, 2 * bands * pairs), F32),
        scratch_shapes=[pltpu.VMEM((bands, right.shape[0], pairs, rows, lanes), BF16)],
        compiler_params=pltpu.CompilerParams(vmem_limit_bytes=VMEM),
        name="finish",
    )(*args)


def swap(value, partner):
    pairs = []
    for b in range(8):
        for d in range(16):
            x, y, z, core = partner(b % 4, (b // 4) * 2 + d // 8, (d // 2) % 4, d % 2)
            pairs.append((b * 16 + d, ((y // 2) * 4 + x) * 16 + (y % 2) * 8 + z * 2 + core))
    return lax.ppermute(value, ("band", "domain"), pairs)


def total_over_cells(partial):
    domains = lax.axis_size("domain")
    half = domains // 2
    groups = [
        [band * domains + y * half + rest for band in range(8) for y in range(2)]
        for rest in range(half)
    ]
    pieces = jnp.broadcast_to(partial[:, None], (8, 2) + partial.shape[1:])
    pieces = pieces.reshape((16,) + partial.shape[1:])
    value = lax.all_to_all(pieces, ("band", "domain"), 0, 0, axis_index_groups=groups).sum(0)
    value = value + swap(value, lambda x, y, z, c: (x, y, z, 1 - c))
    value = value + swap(value, lambda x, y, z, c: (x, y, z ^ 1, c))
    value = value + swap(value, lambda x, y, z, c: (x, y, z ^ 3, c))
    return value


def per_device(orbitals, potential):
    count, nx, ny, nz = orbitals.shape
    cells = float(nx * lax.axis_size("domain") * ny * nz)
    core = (lax.axis_index("domain") % 2).astype(jnp.int32)
    tables = [stage_tables(stage, potential, core, nx // 2) for stage in (1, 2)]
    along_z, along_y, beside, pick = [jnp.asarray(m) for m in block_matrices(ZROWS, ny, count)]
    own = turn(lax.axis_index("band"), core, potential)
    along_z, along_y, beside, pick = [inside(m) for m in (along_z, along_y, beside, pick)]
    early = (own, along_z, along_y, beside, pick)
    half = count // 2
    core = core.reshape(1)

    halos = [edges(core, orbitals, c * half, half) for c in range(2)]
    later = halos[1][1]
    halos = [exchange(*halo) for halo in halos]
    first0, on, off = run_stage(
        1, core, orbitals, *halos[0], tables[0], 0, half, after=(later, *early)
    )
    halos[0] = exchange(on, off)
    first1, on, later = run_stage(1, core, orbitals, *halos[1], tables[0], half, half)
    halos[1] = exchange(on, later)
    (filtered,) = run_stage(
        2, core, first0, *halos[0], tables[1], 0, half, orbitals, after=(later,)
    )
    (filtered,) = run_stage(
        2, core, first1, *halos[1], tables[1], half, half, orbitals, into=filtered
    )
    filtered = inside(lax.all_to_all(filtered, "band", 0, 0))
    on, off, low, high = borders(filtered, pick)
    bands = lax.axis_size("band")
    up = [(i, i + 1) for i in range(bands - 1)]
    below = lax.ppermute(high, "band", up)
    above = lax.ppermute(low, "band", [(target, source) for source, target in up])
    on, off = exchange(on, off)
    applied = local_stage(filtered, own, along_z, along_y)
    sums = gram(1.0 / cells, filtered, applied)
    totals = total_over_cells(finish(1.0 / cells, (below, above, off, on), beside, *sums))
    return (totals[0], totals[1])


def solution(mesh):
    return jax.shard_map(
        per_device,
        mesh=mesh,
        in_specs=(P("band", "domain", None, None), P("domain", None, None)),
        out_specs=(P("band", None), P("band", None)),
        check_vma=False,
    )
```

```python
import functools

import jax
import jax.numpy as jnp
import ml_dtypes
import numpy as np
from jax import lax
from jax.experimental import pallas as pl
from jax.experimental.pallas import tpu as pltpu
from jax.sharding import PartitionSpec as P

COEFS = (
    -5369.0 / 1800.0,
    12.0 / 7.0,
    -15.0 / 56.0,
    10.0 / 189.0,
    -1.0 / 112.0,
    2.0 / 1925.0,
    -1.0 / 16632.0,
)
CENTER = 8.0
HALF = 5.0
REACH = 6
OUTER = (1.0 / HALF, 2.0 / HALF, 1.0)
SHIFT = (-CENTER / HALF, -2.0 * CENTER / HALF, 0.0)
BF16 = jnp.bfloat16
F32 = jnp.float32
ZROWS = 16
NARROW = REACH // 2
SNAKE = (0, 1, 2, 3, 7, 6, 5, 4)
ROWS = 16
VMEM = 12 * 1024 * 1024


def side_weights(stage):
    return [-0.5 * OUTER[stage - 1] * c for c in COEFS]


def band_matrix(stage, size):
    index = np.arange(size)
    gap = np.abs(index[:, None] - index[None, :])
    weights = np.array([0.0] + side_weights(stage)[1:])
    return np.where(gap <= REACH, weights[np.minimum(gap, REACH)], 0.0)


def split_two(matrix):
    high = matrix.astype(ml_dtypes.bfloat16)
    low = (matrix - high.astype(np.float64)).astype(ml_dtypes.bfloat16)
    return high, low


def stencil_matrices(stage, ny, nz, group):
    high, low = split_two(np.kron(np.eye(group), band_matrix(stage, ny)))
    along_y = np.concatenate([high, low], axis=1)
    along_z = np.concatenate(split_two(band_matrix(stage, nz)), axis=0)
    return jnp.asarray(along_y), jnp.asarray(along_z)


def stage_tables(stage, potential, core, group):
    ny, nz = potential.shape[1:]
    own = OUTER[stage - 1] * (potential - 1.5 * COEFS[0]) + SHIFT[stage - 1]
    own = jnp.where(core == 0, own, own[::-1])
    return (own, *stencil_matrices(stage, ny, nz, group))


def stage_body(stage, unused, orbs, first, at, core_ref, *refs):
    width = REACH
    c_ref, off_ref, on_ref, v_ref, my_ref, mz_ref = refs[:6]
    refs = refs[6:]
    if stage == 2:
        o_ref = refs[0]
        refs = refs[1:]
    outs = refs[unused:]
    core = core_ref[0]
    nx, ny, nz = v_ref.shape
    group = my_ref.shape[0] // ny

    def given(ref, b, p, rows):
        return ref[b, p + core * (nx - 1 - 2 * p), rows]

    def center(b, p, rows):
        return given(c_ref, first + b, p, rows) if stage == 1 else c_ref[p, b, rows]

    def beyond(b, i, rows):
        if stage == 1:
            return on_ref[b, i + core * (width - 1 - 2 * i), rows]
        return on_ref[width - 1 - i, b, rows]

    def before(b, i, rows):
        if stage == 1:
            return off_ref[b, (width - 1 - i) + core * (2 * i + 1 - width), rows]
        return off_ref[i, b, rows]

    everything = slice(0, ny)
    side = side_weights(stage)

    def orbital(b):
        lines = [center(b, p, everything) for p in range(nx)]
        sides = [jnp.concatenate(lines[q : q + group], axis=0) for q in range(0, nx, group)]
        part = jnp.concatenate(sides, axis=1)
        flat = jnp.concatenate(sides, axis=0)
        z_term = jnp.dot(
            jnp.concatenate([flat, flat], axis=1), mz_ref[...], preferred_element_type=F32
        ).reshape(nx, ny, nz)
        y_term = jnp.dot(
            my_ref[...], jnp.concatenate([part, part], axis=0), preferred_element_type=F32
        )
        y_parts = [
            y_term[:, k * nz : (k + 1) * nz].reshape(group, ny, nz) for k in range(nx // group)
        ]
        results = {}
        for r in range(0, ny, ROWS):
            rows = slice(r, r + ROWS)
            wide = {}
            for p in range(nx):
                wide[p] = center(b, p, rows).astype(F32)
            for i in range(width):
                wide[-1 - i] = before(b, i, rows).astype(F32)
                wide[nx + i] = beyond(b, i, rows).astype(F32)
            for p in range(nx):
                total = (
                    v_ref[p, rows] * wide[p]
                    + z_term[p, rows]
                    + y_parts[p // group][p % group, rows]
                )
                for s in range(1, REACH + 1):
                    near = []
                    for q in (p - s, p + s):
                        near.append(wide[q])
                    total = total + side[s] * sum(near[1:], near[0])
                if stage == 2:
                    total = total - given(o_ref, first + b, p, rows).astype(F32)
                results[p, r] = total.astype(BF16)
        return results

    if stage == 1:
        for b in range(orbs):
            for (p, r), result in orbital(b).items():
                rows = slice(r, r + ROWS)
                outs[0][p, b, rows] = result
                if p >= nx - REACH:
                    outs[1][p - (nx - REACH), b, rows] = result
                if p < REACH:
                    outs[2][p, b, rows] = result
    else:
        unit = (iota2(nz, 0) == iota2(nz, 1)).astype(F32).astype(BF16)
        for b in range(orbs // 2):
            pair = [orbital(b), orbital(b + orbs // 2)]
            for p in range(nx):
                both = jnp.concatenate(
                    [one[p, r] for one in pair for r in range(0, ny, ROWS)], axis=0
                )
                turned = both.T
                for block, band in enumerate(SNAKE):
                    outs[0][band, p, at + b] = turned[block * ZROWS : (block + 1) * ZROWS]


def iota2(size, dim):
    return lax.broadcasted_iota(jnp.int32, (size, size), dim)


def dot_rows(left, right):
    return lax.dot_general(left, right, (((1,), (1,)), ((), ())), preferred_element_type=F32)


def inside(array):
    return pltpu.with_memory_space_constraint(array, pltpu.VMEM)


def run_stage(stage, core, field, on, off, tables, first, orbs, orbitals=None, after=(), into=None):
    nx, ny, nz = tables[0].shape
    args = [field, off, on, *tables]
    if stage == 2:
        args.append(orbitals)
        count = orbitals.shape[0]
        out_shape = [pltpu.VMEM((nz // ZROWS, nx, count // 2, ZROWS, 2 * ny), BF16)]
    else:
        out_shape = [pltpu.VMEM((n, orbs, ny, nz), BF16) for n in (nx, REACH, REACH)]
    args = [inside(array) for array in args]
    unused = list(after)
    aliases = {}
    vmem = pl.BlockSpec(memory_space=pltpu.VMEM)
    specs = [vmem] * len(args) + [pl.BlockSpec(memory_space=pl.ANY)] * len(unused)
    if into is not None:
        aliases = {1 + len(args): 0}
        unused = [inside(into)] + unused
        specs.insert(len(args), vmem)
    return pl.pallas_call(
        functools.partial(stage_body, stage, len(unused), orbs, first, first // 2),
        in_specs=[pl.BlockSpec(memory_space=pltpu.SMEM)] + specs,
        out_specs=[vmem] * len(out_shape),
        out_shape=out_shape,
        input_output_aliases=aliases,
        compiler_params=pltpu.CompilerParams(vmem_limit_bytes=VMEM),
        cost_estimate=pl.CostEstimate(
            flops=orbs * nx * ny * nz * 1200, bytes_accessed=orbs * nx * ny * nz * 8, transcendentals=0
        ),
        name="stage%d" % stage,
    )(core, *args, *unused)


def edges_body(first, far, core_ref, in_ref, on_ref, off_ref):
    core = core_ref[0]
    for b in range(on_ref.shape[0]):
        on = [in_ref[first + b, i + far * (1 - core)] for i in range(REACH)]
        off = [in_ref[first + b, i + far * core] for i in range(REACH)]
        for i in range(REACH):
            on_ref[b, i] = on[i]
            off_ref[b, i] = off[i]


def edges(core, orbitals, first, orbs):
    nx, ny, nz = orbitals.shape[1:]
    shape = pltpu.VMEM((orbs, REACH, ny, nz), BF16)
    vmem = pl.BlockSpec(memory_space=pltpu.VMEM)
    return pl.pallas_call(
        functools.partial(edges_body, first, nx - REACH),
        in_specs=[pl.BlockSpec(memory_space=pltpu.SMEM), vmem],
        out_specs=[vmem, vmem],
        out_shape=[shape, shape],
        compiler_params=pltpu.CompilerParams(vmem_limit_bytes=VMEM),
        name="edges",
    )(core, inside(orbitals))


def exchange(on, off):
    count = lax.axis_size("domain")
    pairs = [(i, i ^ 1) for i in range(count)]
    facing = [(i, i + 1) for i in range(1, count - 1, 2)]
    facing += [(target, source) for source, target in facing]
    on = lax.ppermute(on, "domain", pairs)
    off = lax.ppermute(off, "domain", facing)
    return on, off


def turn_body(place_ref, v_ref, out_ref, held_ref):
    band, core = place_ref[0], place_ref[1]
    nx = v_ref.shape[0]
    for p in range(nx):
        line = v_ref[p + core * (nx - 1 - 2 * p)] - 1.5 * COEFS[0]
        held_ref[p] = jnp.concatenate([line, line], axis=0).T
    for p in range(nx):
        out_ref[p] = held_ref[p, pl.ds(pl.multiple_of(band * ZROWS, ZROWS), ZROWS), :]


def turn(band, core, potential):
    nx, ny, nz = potential.shape
    vmem = pl.BlockSpec(memory_space=pltpu.VMEM)
    return pl.pallas_call(
        turn_body,
        in_specs=[pl.BlockSpec(memory_space=pltpu.SMEM), vmem],
        out_specs=vmem,
        out_shape=pltpu.VMEM((nx, ZROWS, 2 * ny), F32),
        scratch_shapes=[pltpu.VMEM((nx, nz, 2 * ny), F32)],
        compiler_params=pltpu.CompilerParams(vmem_limit_bytes=VMEM),
        name="turn",
    )(jnp.stack([band, core]).astype(jnp.int32), inside(potential))


def block_matrices(nz_block, ny, blocks):
    side = side_weights(3)
    reach = NARROW
    low, high = np.zeros((nz_block, reach)), np.zeros((nz_block, reach))
    for i in range(nz_block):
        for j in range(reach):
            gap = i + reach - j
            if gap <= REACH:
                low[i, j] = side[gap] * (1 if i < reach else 2)
            gap = nz_block - i + j
            if gap <= REACH:
                high[i, j] = side[gap] * (1 if nz_block - 1 - i < reach else 2)
    unit = np.eye(blocks)
    own = split_two(np.kron(unit, band_matrix(3, nz_block)))
    beside = split_two(np.concatenate([np.kron(unit, low), np.kron(unit, high)], axis=1))
    along_z, beside = np.concatenate(own, axis=1), np.concatenate(beside, axis=1)
    twice = np.kron(np.eye(2), band_matrix(3, ny))
    along_y = np.concatenate(split_two(twice), axis=0)
    pick = np.zeros((2, reach, nz_block))
    for j in range(reach):
        pick[0, j, j] = 1
        pick[1, j, nz_block - reach + j] = 1
    pick = np.concatenate([np.kron(unit, pick[0]), np.kron(unit, pick[1])], axis=0)
    return along_z, along_y, beside, pick.astype(ml_dtypes.bfloat16)


def two_planes(ref, s, p):
    pairs, rows, lanes = ref.shape[2:]
    return jnp.concatenate([ref[s, p + i].reshape(pairs * rows, lanes) for i in range(2)], axis=0)


def borders_body(f_ref, pick_ref, on_ref, off_ref, low_ref, high_ref):
    bands, nx = f_ref.shape[:2]
    count = low_ref.shape[2]
    for s in range(bands):
        for p in range(0, nx, 2):
            rows = jnp.dot(pick_ref[...], two_planes(f_ref, s, p), preferred_element_type=F32)
            rows = rows.astype(BF16)
            low_ref[s, p // 2] = rows[:count]
            high_ref[s, p // 2] = rows[count:]
        for p in range(NARROW):
            off_ref[s, p] = f_ref[s, p]
            on_ref[s, p] = f_ref[s, nx - NARROW + p]


def borders(filtered, pick):
    bands, nx, pairs, rows, lanes = filtered.shape
    vmem = pl.BlockSpec(memory_space=pltpu.VMEM)
    planes = pltpu.VMEM((bands, NARROW, pairs, rows, lanes), BF16)
    lines = pltpu.VMEM((bands, nx // 2, pick.shape[0] // 2, lanes), BF16)
    return pl.pallas_call(
        borders_body,
        in_specs=[vmem, vmem],
        out_specs=[vmem] * 4,
        out_shape=[planes, planes, lines, lines],
        compiler_params=pltpu.CompilerParams(vmem_limit_bytes=VMEM),
        name="borders",
    )(filtered, inside(pick))


def local_body(f_ref, v_ref, mz_ref, my_ref, out_ref):
    bands, nx, pairs, rows, lanes = f_ref.shape
    side = side_weights(3)
    for s in range(bands):
        z_terms, y_terms = [], []
        for p in range(0, nx, 4):
            data = jnp.concatenate([two_planes(f_ref, s, p + i) for i in (0, 2)], axis=1)
            term = jnp.dot(
                mz_ref[...], jnp.concatenate([data, data], axis=0), preferred_element_type=F32
            )
            for i in range(2):
                half = term[:, i * lanes : (i + 1) * lanes].reshape(2, pairs, rows, lanes)
                z_terms += [half[0], half[1]]
        for p in range(0, nx, 2):
            data = two_planes(f_ref, s, p)
            term = jnp.dot(
                jnp.concatenate([data, data], axis=1), my_ref[...], preferred_element_type=F32
            ).reshape(2, pairs, rows, lanes)
            y_terms += [term[0], term[1]]
        results = {}
        for q in range(pairs):
            wide = [f_ref[s, p, q].astype(F32) for p in range(nx)]
            for p in range(nx):
                total = v_ref[p] * wide[p] + z_terms[p][q] + y_terms[p][q]
                for gap in range(1, REACH + 1):
                    near = [wide[other] for other in (p - gap, p + gap) if 0 <= other < nx]
                    if near:
                        total = total + side[gap] * sum(near[1:], near[0])
                results[p, q] = total.astype(BF16)
        for (p, q), result in results.items():
            out_ref[s, p, q] = result


def local_stage(filtered, own, along_z, along_y):
    vmem = pl.BlockSpec(memory_space=pltpu.VMEM)
    args = [inside(array) for array in (filtered, own, along_z, along_y)]
    return pl.pallas_call(
        local_body,
        in_specs=[vmem] * len(args),
        out_specs=vmem,
        out_shape=pltpu.VMEM(filtered.shape, BF16),
        compiler_params=pltpu.CompilerParams(vmem_limit_bytes=VMEM),
        cost_estimate=pl.CostEstimate(flops=10**9, bytes_accessed=2**22, transcendentals=0),
        name="local",
    )(*args)


def orbital_rows(block):
    count, rows, lanes = block.shape
    half = lanes // 2
    change = iota2(lanes, 0) == (iota2(lanes, 1) + half) % lanes
    change = change.astype(F32).astype(BF16)
    block = jnp.swapaxes(block, 0, 1)
    changed = jnp.dot(block.reshape(rows * count, lanes), change, preferred_element_type=F32)
    changed = changed.astype(BF16).reshape(rows, count, lanes)
    first = lax.broadcasted_iota(jnp.int32, (count, lanes), 1) < half
    parts = []
    for z in range(0, rows, 2):
        even = jnp.where(first, block[z], changed[z + 1])
        odd = jnp.where(first, changed[z], block[z + 1])
        parts.append(jnp.concatenate([even, odd], axis=0))
    return [jnp.concatenate(parts[i : i + 2], axis=1) for i in range(0, len(parts), 2)]


def natural_rows(square, pairs):
    size = square.shape[0]
    four = pairs // 2
    parts = []
    for row in range(0, size, four):
        band, chunk, half = row // (4 * four), (row // (2 * four)) % 2, (row // four) % 2
        start = half * (size // 2) + band * pairs + chunk * four
        parts.append(square[start : start + four])
    return jnp.concatenate(parts, axis=0)


def gram_body(scale, f_ref, a_ref, corr_ref, total_ref, right_ref):
    bands, nx, pairs, rows, lanes = f_ref.shape
    count = bands * pairs

    def block(p, total):
        right = orbital_rows(f_ref[:, p].reshape(count, rows, lanes))
        left = orbital_rows(a_ref[:, p].reshape(count, rows, lanes))
        for i, (one, other) in enumerate(zip(right, left)):
            right_ref[p, i] = one
            total = total + dot_rows(jnp.concatenate([one, other], axis=0), one)
        return total

    total = jnp.zeros((4 * count, 2 * count), F32)
    for p in range(nx):
        total = block(p, total)
    total_ref[...] = total[2 * count :]
    corr = natural_rows(total[: 2 * count] * scale, pairs).T
    corr_ref[...] = natural_rows(corr, pairs)


def gram(scale, filtered, applied):
    bands, nx, pairs, rows, lanes = filtered.shape
    size = 2 * bands * pairs
    vmem = pl.BlockSpec(memory_space=pltpu.VMEM)
    return pl.pallas_call(
        functools.partial(gram_body, scale),
        in_specs=[vmem, vmem],
        out_specs=[vmem] * 3,
        out_shape=[
            pltpu.VMEM((size, size), F32),
            pltpu.VMEM((size, size), F32),
            pltpu.VMEM((nx, rows // 4, size, 2 * lanes), BF16),
        ],
        compiler_params=pltpu.CompilerParams(vmem_limit_bytes=3 * VMEM),
        cost_estimate=pl.CostEstimate(flops=10**9, bytes_accessed=2**22, transcendentals=0),
        name="gram",
    )(inside(filtered), inside(applied))


def finish_body(
    scale,
    low_ref,
    high_ref,
    off_ref,
    on_ref,
    beside_ref,
    corr_ref,
    total_ref,
    right_ref,
    out_ref,
    cross_ref,
):
    bands, width, pairs, rows, lanes = off_ref.shape
    nx = right_ref.shape[0]
    count = bands * pairs
    side = side_weights(3)
    for s in range(bands):
        z_terms = []
        for p in range(0, nx, 4):
            halo = jnp.concatenate(
                [
                    jnp.concatenate([low_ref[s, p // 2 + i], high_ref[s, p // 2 + i]], axis=0)
                    for i in range(2)
                ],
                axis=1,
            )
            term = jnp.dot(
                beside_ref[...],
                jnp.concatenate([halo, halo], axis=0),
                preferred_element_type=F32,
            )
            for i in range(2):
                half = term[:, i * lanes : (i + 1) * lanes].reshape(2, pairs, rows, lanes)
                z_terms += [half[0], half[1]]
        for q in range(pairs):
            off = [off_ref[s, i, q].astype(F32) for i in range(width)]
            on = [on_ref[s, width - 1 - i, q].astype(F32) for i in range(width)]
            for p in range(nx):
                total = z_terms[p][q]
                for beyond, depth in ((off, p), (on, nx - 1 - p)):
                    weight = 2.0 if depth >= width else 1.0
                    for i in range(width):
                        if depth + i + 1 <= REACH:
                            total = total + (weight * side[depth + i + 1]) * beyond[i]
                cross_ref[s, p, q] = total.astype(BF16)

    def block(p, total):
        left = orbital_rows(cross_ref[:, p].reshape(count, rows, lanes))
        for i, one in enumerate(left):
            total = total + dot_rows(one, right_ref[p, i])
        return total

    proj = total_ref[...]
    for p in range(nx):
        proj = block(p, proj)
    proj = natural_rows((0.5 * scale) * (proj + proj.T), pairs).T
    proj = natural_rows(proj, pairs)
    size = 2 * pairs
    for band in range(bands):
        out_ref[band, 0] = corr_ref[band * size : (band + 1) * size]
        out_ref[band, 1] = proj[band * size : (band + 1) * size]


def finish(scale, halos, beside, corr, total, right):
    bands, _, pairs, rows, lanes = halos[2].shape
    vmem = pl.BlockSpec(memory_space=pltpu.VMEM)
    args = [inside(array) for array in (*halos, beside, corr, total, right)]
    return pl.pallas_call(
        functools.partial(finish_body, scale),
        in_specs=[vmem] * len(args),
        out_specs=vmem,
        out_shape=jax.ShapeDtypeStruct((bands, 2, 2 * pairs, 2 * bands * pairs), F32),
        scratch_shapes=[pltpu.VMEM((bands, right.shape[0], pairs, rows, lanes), BF16)],
        compiler_params=pltpu.CompilerParams(vmem_limit_bytes=3 * VMEM),
        name="finish",
    )(*args)


def swap(value, partner):
    pairs = []
    for b in range(8):
        for d in range(16):
            x, y, z, core = partner(b % 4, (b // 4) * 2 + d // 8, (d // 2) % 4, d % 2)
            pairs.append((b * 16 + d, ((y // 2) * 4 + x) * 16 + (y % 2) * 8 + z * 2 + core))
    return lax.ppermute(value, ("band", "domain"), pairs)


def total_over_cells(partial):
    domains = lax.axis_size("domain")
    half = domains // 2
    groups = [
        [band * domains + y * half + rest for band in range(8) for y in range(2)]
        for rest in range(half)
    ]
    pieces = jnp.broadcast_to(partial[:, None], (8, 2) + partial.shape[1:])
    pieces = pieces.reshape((16,) + partial.shape[1:])
    value = lax.all_to_all(pieces, ("band", "domain"), 0, 0, axis_index_groups=groups).sum(0)
    value = value + swap(value, lambda x, y, z, c: (x, y, z, 1 - c))
    value = value + swap(value, lambda x, y, z, c: (x, y, z ^ 1, c))
    value = value + swap(value, lambda x, y, z, c: (x, y, z ^ 3, c))
    return value


def per_device(orbitals, potential):
    count, nx, ny, nz = orbitals.shape
    cells = float(nx * lax.axis_size("domain") * ny * nz)
    core = (lax.axis_index("domain") % 2).astype(jnp.int32)
    tables = [stage_tables(stage, potential, core, nx // 2) for stage in (1, 2)]
    along_z, along_y, beside, pick = [jnp.asarray(m) for m in block_matrices(ZROWS, ny, count)]
    band = lax.axis_index("band")
    own = turn(jnp.where(band < 4, band, 11 - band), core, potential)
    along_z, along_y, beside, pick = [inside(m) for m in (along_z, along_y, beside, pick)]
    early = (own, along_z, along_y, beside, pick)
    half = count // 2
    core = core.reshape(1)

    halos = [edges(core, orbitals, c * half, half) for c in range(2)]
    later = halos[1][1]
    halos = [exchange(*halo) for halo in halos]
    first0, on, off = run_stage(
        1, core, orbitals, *halos[0], tables[0], 0, half, after=(later, *early)
    )
    halos[0] = exchange(on, off)
    first1, on, later = run_stage(1, core, orbitals, *halos[1], tables[0], half, half)
    halos[1] = exchange(on, later)
    (filtered,) = run_stage(
        2, core, first0, *halos[0], tables[1], 0, half, orbitals, after=(later,)
    )
    (filtered,) = run_stage(
        2, core, first1, *halos[1], tables[1], half, half, orbitals, into=filtered
    )
    filtered = inside(lax.all_to_all(filtered, "band", 0, 0))
    on, off, low, high = borders(filtered, pick)
    up = list(zip(SNAKE[:-1], SNAKE[1:]))
    below = lax.ppermute(high, "band", up)
    above = lax.ppermute(low, "band", [(target, source) for source, target in up])
    on, off = exchange(on, off)
    applied = local_stage(filtered, own, along_z, along_y)
    sums = gram(1.0 / cells, filtered, applied)
    totals = total_over_cells(finish(1.0 / cells, (below, above, off, on), beside, *sums))
    return (totals[0], totals[1])


def solution(mesh):
    return jax.shard_map(
        per_device,
        mesh=mesh,
        in_specs=(P("band", "domain", None, None), P("domain", None, None)),
        out_specs=(P("band", None), P("band", None)),
        check_vma=False,
    )
```

```python
import functools

import jax
import jax.numpy as jnp
import ml_dtypes
import numpy as np
from jax import lax
from jax.experimental import pallas as pl
from jax.experimental.pallas import tpu as pltpu
from jax.sharding import PartitionSpec as P

COEFS = (
    -5369.0 / 1800.0,
    12.0 / 7.0,
    -15.0 / 56.0,
    10.0 / 189.0,
    -1.0 / 112.0,
    2.0 / 1925.0,
    -1.0 / 16632.0,
)
CENTER = 8.0
HALF = 5.0
REACH = 6
OUTER = (1.0 / HALF, 2.0 / HALF, 1.0)
SHIFT = (-CENTER / HALF, -2.0 * CENTER / HALF, 0.0)
BF16 = jnp.bfloat16
F32 = jnp.float32
ZROWS = 16
NARROW = REACH // 2
SNAKE = (0, 1, 2, 3, 7, 6, 5, 4)
ROWS = 16
VMEM = 12 * 1024 * 1024


def side_weights(stage):
    return [-0.5 * OUTER[stage - 1] * c for c in COEFS]


def band_matrix(stage, size):
    index = np.arange(size)
    gap = np.abs(index[:, None] - index[None, :])
    weights = np.array([0.0] + side_weights(stage)[1:])
    return np.where(gap <= REACH, weights[np.minimum(gap, REACH)], 0.0)


def split_two(matrix):
    high = matrix.astype(ml_dtypes.bfloat16)
    low = (matrix - high.astype(np.float64)).astype(ml_dtypes.bfloat16)
    return high, low


def stencil_matrices(stage, ny, nz, group):
    high, low = split_two(np.kron(np.eye(group), band_matrix(stage, ny)))
    along_y = np.concatenate([high, low], axis=1)
    along_z = np.concatenate(split_two(band_matrix(stage, nz)), axis=0)
    return jnp.asarray(along_y), jnp.asarray(along_z)


def stage_tables(stage, potential, core, group):
    ny, nz = potential.shape[1:]
    own = OUTER[stage - 1] * (potential - 1.5 * COEFS[0]) + SHIFT[stage - 1]
    own = jnp.where(core == 0, own, own[::-1])
    return (own, *stencil_matrices(stage, ny, nz, group))


def stage_body(stage, unused, orbs, first, at, *refs):
    width = REACH
    c_ref, off_ref, on_ref, v_ref, my_ref, mz_ref = refs[:6]
    refs = refs[6:]
    if stage == 2:
        o_ref = refs[0]
        refs = refs[1:]
    outs = refs[unused:]
    core = this_core()
    nx, ny, nz = v_ref.shape
    group = my_ref.shape[0] // ny

    def given(ref, b, p, rows):
        return ref[b, p + core * (nx - 1 - 2 * p), rows]

    def center(b, p, rows):
        return given(c_ref, first + b, p, rows) if stage == 1 else c_ref[p, b, rows]

    def beyond(b, i, rows):
        if stage == 1:
            return on_ref[b, i + core * (width - 1 - 2 * i), rows]
        return on_ref[width - 1 - i, b, rows]

    def before(b, i, rows):
        if stage == 1:
            return off_ref[b, (width - 1 - i) + core * (2 * i + 1 - width), rows]
        return off_ref[i, b, rows]

    everything = slice(0, ny)
    side = side_weights(stage)

    def orbital(b):
        lines = [center(b, p, everything) for p in range(nx)]
        sides = [jnp.concatenate(lines[q : q + group], axis=0) for q in range(0, nx, group)]
        part = jnp.concatenate(sides, axis=1)
        flat = jnp.concatenate(sides, axis=0)
        z_term = jnp.dot(
            jnp.concatenate([flat, flat], axis=1), mz_ref[...], preferred_element_type=F32
        ).reshape(nx, ny, nz)
        y_term = jnp.dot(
            my_ref[...], jnp.concatenate([part, part], axis=0), preferred_element_type=F32
        )
        y_parts = [
            y_term[:, k * nz : (k + 1) * nz].reshape(group, ny, nz) for k in range(nx // group)
        ]
        results = {}
        for r in range(0, ny, ROWS):
            rows = slice(r, r + ROWS)
            wide = {}
            for p in range(nx):
                wide[p] = center(b, p, rows).astype(F32)
            for i in range(width):
                wide[-1 - i] = before(b, i, rows).astype(F32)
                wide[nx + i] = beyond(b, i, rows).astype(F32)
            for p in range(nx):
                total = (
                    v_ref[p, rows] * wide[p]
                    + z_term[p, rows]
                    + y_parts[p // group][p % group, rows]
                )
                for s in range(1, REACH + 1):
                    near = []
                    for q in (p - s, p + s):
                        near.append(wide[q])
                    total = total + side[s] * sum(near[1:], near[0])
                if stage == 2:
                    total = total - given(o_ref, first + b, p, rows).astype(F32)
                results[p, r] = total.astype(BF16)
        return results

    if stage == 1:
        for b in range(orbs):
            for (p, r), result in orbital(b).items():
                rows = slice(r, r + ROWS)
                outs[0][p, b, rows] = result
                if p >= nx - REACH:
                    outs[1][p - (nx - REACH), b, rows] = result
                if p < REACH:
                    outs[2][p, b, rows] = result
    else:
        for b in range(orbs // 2):
            pair = [orbital(b), orbital(b + orbs // 2)]
            for p in range(nx):
                both = jnp.concatenate(
                    [one[p, r] for one in pair for r in range(0, ny, ROWS)], axis=0
                )
                turned = both.T
                for block, band in enumerate(SNAKE):
                    outs[0][band, p, at + b] = turned[block * ZROWS : (block + 1) * ZROWS]


def iota2(size, dim):
    return lax.broadcasted_iota(jnp.int32, (size, size), dim)


def dot_rows(left, right):
    return lax.dot_general(left, right, (((1,), (1,)), ((), ())), preferred_element_type=F32)


def inside(array):
    return pltpu.with_memory_space_constraint(array, pltpu.VMEM)


def run_stage(stage, field, on, off, tables, first, orbs, orbitals=None, after=(), into=None):
    nx, ny, nz = tables[0].shape
    args = [field, off, on, *tables]
    if stage == 2:
        args.append(orbitals)
        count = orbitals.shape[0]
        out_shape = [pltpu.VMEM((nz // ZROWS, nx, count // 2, ZROWS, 2 * ny), BF16)]
    else:
        out_shape = [pltpu.VMEM((n, orbs, ny, nz), BF16) for n in (nx, REACH, REACH)]
    args = [inside(array) for array in args]
    unused = list(after)
    aliases = {}
    vmem = pl.BlockSpec(memory_space=pltpu.VMEM)
    specs = [vmem] * len(args) + [pl.BlockSpec(memory_space=pl.ANY)] * len(unused)
    if into is not None:
        aliases = {len(args): 0}
        unused = [inside(into)] + unused
        specs.insert(len(args), vmem)
    return pl.pallas_call(
        functools.partial(stage_body, stage, len(unused), orbs, first, first // 2),
        in_specs=specs,
        out_specs=[vmem] * len(out_shape),
        out_shape=out_shape,
        input_output_aliases=aliases,
        compiler_params=pltpu.CompilerParams(vmem_limit_bytes=VMEM),
        cost_estimate=pl.CostEstimate(
            flops=orbs * nx * ny * nz * 1200, bytes_accessed=orbs * nx * ny * nz * 8, transcendentals=0
        ),
        name="stage%d" % stage,
    )(*args, *unused)


def edges_body(first, far, in_ref, on_ref, off_ref):
    own = this_core()
    for core in range(2):

        @pl.when(own == core)
        def _():
            for b in range(on_ref.shape[0]):
                on = [in_ref[first + b, i + far * (1 - core)] for i in range(REACH)]
                off = [in_ref[first + b, i + far * core] for i in range(REACH)]
                for i in range(REACH):
                    on_ref[b, i] = on[i]
                    off_ref[b, i] = off[i]


def edges(orbitals, first, orbs):
    nx, ny, nz = orbitals.shape[1:]
    shape = pltpu.VMEM((orbs, REACH, ny, nz), BF16)
    vmem = pl.BlockSpec(memory_space=pltpu.VMEM)
    return pl.pallas_call(
        functools.partial(edges_body, first, nx - REACH),
        in_specs=[vmem],
        out_specs=[vmem, vmem],
        out_shape=[shape, shape],
        compiler_params=pltpu.CompilerParams(vmem_limit_bytes=VMEM),
        name="edges",
    )(inside(orbitals))


def exchange(on, off):
    count = lax.axis_size("domain")
    pairs = [(i, i ^ 1) for i in range(count)]
    facing = [(i, i + 1) for i in range(1, count - 1, 2)]
    facing += [(target, source) for source, target in facing]
    on = lax.ppermute(on, "domain", pairs)
    off = lax.ppermute(off, "domain", facing)
    return on, off


def this_core():
    return lax.axis_index("domain") % 2


def turn_body(v_ref, out_ref, held_ref):
    core = this_core()
    band = lax.axis_index("band")
    block = jnp.where(band < 4, band, 11 - band)
    nx = v_ref.shape[0]
    for p in range(nx):
        line = v_ref[p + core * (nx - 1 - 2 * p)] - 1.5 * COEFS[0]
        held_ref[p] = jnp.concatenate([line, line], axis=0).T
    for p in range(nx):
        out_ref[p] = held_ref[p, pl.ds(pl.multiple_of(block * ZROWS, ZROWS), ZROWS), :]


def turn(potential):
    nx, ny, nz = potential.shape
    vmem = pl.BlockSpec(memory_space=pltpu.VMEM)
    return pl.pallas_call(
        turn_body,
        in_specs=[vmem],
        out_specs=vmem,
        out_shape=pltpu.VMEM((nx, ZROWS, 2 * ny), F32),
        scratch_shapes=[pltpu.VMEM((nx, nz, 2 * ny), F32)],
        compiler_params=pltpu.CompilerParams(vmem_limit_bytes=VMEM),
        name="turn",
    )(inside(potential))


def block_matrices(nz_block, ny, blocks):
    side = side_weights(3)
    reach = NARROW
    low, high = np.zeros((nz_block, reach)), np.zeros((nz_block, reach))
    for i in range(nz_block):
        for j in range(reach):
            gap = i + reach - j
            if gap <= REACH:
                low[i, j] = side[gap] * (1 if i < reach else 2)
            gap = nz_block - i + j
            if gap <= REACH:
                high[i, j] = side[gap] * (1 if nz_block - 1 - i < reach else 2)
    unit = np.eye(blocks)
    own = split_two(np.kron(unit, band_matrix(3, nz_block)))
    beside = split_two(np.concatenate([np.kron(unit, low), np.kron(unit, high)], axis=1))
    along_z, beside = np.concatenate(own, axis=1), np.concatenate(beside, axis=1)
    twice = np.kron(np.eye(2), band_matrix(3, ny))
    along_y = np.concatenate(split_two(twice), axis=0)
    pick = np.zeros((2, reach, nz_block))
    for j in range(reach):
        pick[0, j, j] = 1
        pick[1, j, nz_block - reach + j] = 1
    pick = np.concatenate([np.kron(unit, pick[0]), np.kron(unit, pick[1])], axis=0)
    return along_z, along_y, beside, pick.astype(ml_dtypes.bfloat16)


def two_planes(ref, s, p):
    pairs, rows, lanes = ref.shape[2:]
    return jnp.concatenate([ref[s, p + i].reshape(pairs * rows, lanes) for i in range(2)], axis=0)


def lines_body(f_ref, pick_ref, low_ref, high_ref):
    bands, nx = f_ref.shape[:2]
    count = low_ref.shape[2]
    for s in range(bands):
        for p in range(0, nx, 2):
            rows = jnp.dot(pick_ref[...], two_planes(f_ref, s, p), preferred_element_type=F32)
            rows = rows.astype(BF16)
            low_ref[s, p // 2] = rows[:count]
            high_ref[s, p // 2] = rows[count:]


def border_lines(filtered, pick):
    bands, nx, pairs, rows, lanes = filtered.shape
    vmem = pl.BlockSpec(memory_space=pltpu.VMEM)
    lines = pltpu.VMEM((bands, nx // 2, pick.shape[0] // 2, lanes), BF16)
    return pl.pallas_call(
        lines_body,
        in_specs=[vmem, vmem],
        out_specs=[vmem] * 2,
        out_shape=[lines, lines],
        compiler_params=pltpu.CompilerParams(vmem_limit_bytes=VMEM),
        name="lines",
    )(filtered, inside(pick))


def planes_body(f_ref, after_ref, on_ref, off_ref):
    bands, nx = f_ref.shape[:2]
    for s in range(bands):
        for p in range(NARROW):
            off_ref[s, p] = f_ref[s, p]
            on_ref[s, p] = f_ref[s, nx - NARROW + p]


def border_planes(filtered, after):
    bands, nx, pairs, rows, lanes = filtered.shape
    vmem = pl.BlockSpec(memory_space=pltpu.VMEM)
    planes = pltpu.VMEM((bands, NARROW, pairs, rows, lanes), BF16)
    return pl.pallas_call(
        planes_body,
        in_specs=[vmem, pl.BlockSpec(memory_space=pl.ANY)],
        out_specs=[vmem] * 2,
        out_shape=[planes, planes],
        compiler_params=pltpu.CompilerParams(vmem_limit_bytes=VMEM),
        name="planes",
    )(filtered, after)


def local_body(f_ref, v_ref, mz_ref, my_ref, out_ref):
    bands, nx, pairs, rows, lanes = f_ref.shape
    side = side_weights(3)
    for s in range(bands):
        z_terms, y_terms = [], []
        for p in range(0, nx, 4):
            data = jnp.concatenate([two_planes(f_ref, s, p + i) for i in (0, 2)], axis=1)
            term = jnp.dot(
                mz_ref[...], jnp.concatenate([data, data], axis=0), preferred_element_type=F32
            )
            for i in range(2):
                half = term[:, i * lanes : (i + 1) * lanes].reshape(2, pairs, rows, lanes)
                z_terms += [half[0], half[1]]
        for p in range(0, nx, 2):
            data = two_planes(f_ref, s, p)
            term = jnp.dot(
                jnp.concatenate([data, data], axis=1), my_ref[...], preferred_element_type=F32
            ).reshape(2, pairs, rows, lanes)
            y_terms += [term[0], term[1]]
        results = {}
        for q in range(pairs):
            wide = [f_ref[s, p, q].astype(F32) for p in range(nx)]
            for p in range(nx):
                total = v_ref[p] * wide[p] + z_terms[p][q] + y_terms[p][q]
                for gap in range(1, REACH + 1):
                    near = [wide[other] for other in (p - gap, p + gap) if 0 <= other < nx]
                    if near:
                        total = total + side[gap] * sum(near[1:], near[0])
                results[p, q] = total.astype(BF16)
        for (p, q), result in results.items():
            out_ref[s, p, q] = result


def local_stage(filtered, own, along_z, along_y):
    vmem = pl.BlockSpec(memory_space=pltpu.VMEM)
    args = [inside(array) for array in (filtered, own, along_z, along_y)]
    return pl.pallas_call(
        local_body,
        in_specs=[vmem] * len(args),
        out_specs=vmem,
        out_shape=pltpu.VMEM(filtered.shape, BF16),
        compiler_params=pltpu.CompilerParams(vmem_limit_bytes=VMEM),
        cost_estimate=pl.CostEstimate(flops=10**9, bytes_accessed=2**22, transcendentals=0),
        name="local",
    )(*args)


def orbital_rows(block):
    count, rows, lanes = block.shape
    half = lanes // 2
    change = iota2(lanes, 0) == (iota2(lanes, 1) + half) % lanes
    change = change.astype(F32).astype(BF16)
    block = jnp.swapaxes(block, 0, 1)
    changed = jnp.dot(block.reshape(rows * count, lanes), change, preferred_element_type=F32)
    changed = changed.astype(BF16).reshape(rows, count, lanes)
    first = lax.broadcasted_iota(jnp.int32, (count, lanes), 1) < half
    parts = []
    for z in range(0, rows, 2):
        even = jnp.where(first, block[z], changed[z + 1])
        odd = jnp.where(first, changed[z], block[z + 1])
        parts.append(jnp.concatenate([even, odd], axis=0))
    return [jnp.concatenate(parts[i : i + 2], axis=1) for i in range(0, len(parts), 2)]


def natural_rows(square, pairs):
    size = square.shape[0]
    four = pairs // 2
    parts = []
    for row in range(0, size, four):
        band, chunk, half = row // (4 * four), (row // (2 * four)) % 2, (row // four) % 2
        start = half * (size // 2) + band * pairs + chunk * four
        parts.append(square[start : start + four])
    return jnp.concatenate(parts, axis=0)


def gram_body(scale, f_ref, a_ref, corr_ref, total_ref, right_ref):
    bands, nx, pairs, rows, lanes = f_ref.shape
    count = bands * pairs

    def block(p, total):
        right = orbital_rows(f_ref[:, p].reshape(count, rows, lanes))
        left = orbital_rows(a_ref[:, p].reshape(count, rows, lanes))
        for i, (one, other) in enumerate(zip(right, left)):
            right_ref[p, i] = one
            total = total + dot_rows(jnp.concatenate([one, other], axis=0), one)
        return total

    total = jnp.zeros((4 * count, 2 * count), F32)
    for p in range(nx):
        total = block(p, total)
    total_ref[...] = total[2 * count :]
    corr = natural_rows(total[: 2 * count] * scale, pairs).T
    corr_ref[...] = natural_rows(corr, pairs)


def gram(scale, filtered, applied):
    bands, nx, pairs, rows, lanes = filtered.shape
    size = 2 * bands * pairs
    vmem = pl.BlockSpec(memory_space=pltpu.VMEM)
    return pl.pallas_call(
        functools.partial(gram_body, scale),
        in_specs=[vmem, vmem],
        out_specs=[vmem] * 3,
        out_shape=[
            pltpu.VMEM((size, size), F32),
            pltpu.VMEM((size, size), F32),
            pltpu.VMEM((nx, rows // 4, size, 2 * lanes), BF16),
        ],
        compiler_params=pltpu.CompilerParams(vmem_limit_bytes=3 * VMEM),
        cost_estimate=pl.CostEstimate(flops=10**9, bytes_accessed=2**22, transcendentals=0),
        name="gram",
    )(inside(filtered), inside(applied))


def finish_body(
    scale,
    low_ref,
    high_ref,
    off_ref,
    on_ref,
    beside_ref,
    corr_ref,
    total_ref,
    right_ref,
    out_ref,
    cross_ref,
):
    bands, width, pairs, rows, lanes = off_ref.shape
    nx = right_ref.shape[0]
    count = bands * pairs
    side = side_weights(3)
    for s in range(bands):
        z_terms = []
        for p in range(0, nx, 4):
            halo = jnp.concatenate(
                [
                    jnp.concatenate([low_ref[s, p // 2 + i], high_ref[s, p // 2 + i]], axis=0)
                    for i in range(2)
                ],
                axis=1,
            )
            term = jnp.dot(
                beside_ref[...],
                jnp.concatenate([halo, halo], axis=0),
                preferred_element_type=F32,
            )
            for i in range(2):
                half = term[:, i * lanes : (i + 1) * lanes].reshape(2, pairs, rows, lanes)
                z_terms += [half[0], half[1]]
        for q in range(pairs):
            off = [off_ref[s, i, q].astype(F32) for i in range(width)]
            on = [on_ref[s, width - 1 - i, q].astype(F32) for i in range(width)]
            for p in range(nx):
                total = z_terms[p][q]
                for beyond, depth in ((off, p), (on, nx - 1 - p)):
                    weight = 2.0 if depth >= width else 1.0
                    for i in range(width):
                        if depth + i + 1 <= REACH:
                            total = total + (weight * side[depth + i + 1]) * beyond[i]
                cross_ref[s, p, q] = total.astype(BF16)

    def block(p, total):
        left = orbital_rows(cross_ref[:, p].reshape(count, rows, lanes))
        for i, one in enumerate(left):
            total = total + dot_rows(one, right_ref[p, i])
        return total

    proj = total_ref[...]
    for p in range(nx):
        proj = block(p, proj)
    proj = natural_rows((0.5 * scale) * (proj + proj.T), pairs).T
    proj = natural_rows(proj, pairs)
    size = 2 * pairs
    for band in range(bands):
        out_ref[band, 0] = corr_ref[band * size : (band + 1) * size]
        out_ref[band, 1] = proj[band * size : (band + 1) * size]


def finish(scale, halos, beside, corr, total, right):
    bands, _, pairs, rows, lanes = halos[2].shape
    vmem = pl.BlockSpec(memory_space=pltpu.VMEM)
    args = [inside(array) for array in (*halos, beside, corr, total, right)]
    return pl.pallas_call(
        functools.partial(finish_body, scale),
        in_specs=[vmem] * len(args),
        out_specs=vmem,
        out_shape=jax.ShapeDtypeStruct((bands, 2, 2 * pairs, 2 * bands * pairs), F32),
        scratch_shapes=[pltpu.VMEM((bands, right.shape[0], pairs, rows, lanes), BF16)],
        compiler_params=pltpu.CompilerParams(vmem_limit_bytes=3 * VMEM),
        name="finish",
    )(*args)


def swap(value, partner):
    pairs = []
    for b in range(8):
        for d in range(16):
            x, y, z, core = partner(b % 4, (b // 4) * 2 + d // 8, (d // 2) % 4, d % 2)
            pairs.append((b * 16 + d, ((y // 2) * 4 + x) * 16 + (y % 2) * 8 + z * 2 + core))
    return lax.ppermute(value, ("band", "domain"), pairs)


def total_over_cells(partial):
    domains = lax.axis_size("domain")
    half = domains // 2
    groups = [
        [band * domains + y * half + rest for band in range(8) for y in range(2)]
        for rest in range(half)
    ]
    pieces = jnp.broadcast_to(partial[:, None], (8, 2) + partial.shape[1:])
    pieces = pieces.reshape((16,) + partial.shape[1:])
    value = lax.all_to_all(pieces, ("band", "domain"), 0, 0, axis_index_groups=groups).sum(0)
    value = value + swap(value, lambda x, y, z, c: (x, y, z, 1 - c))
    value = value + swap(value, lambda x, y, z, c: (x, y, z ^ 1, c))
    value = value + swap(value, lambda x, y, z, c: (x, y, z ^ 3, c))
    return value


def per_device(orbitals, potential):
    count, nx, ny, nz = orbitals.shape
    cells = float(nx * lax.axis_size("domain") * ny * nz)
    core = this_core()
    tables = [stage_tables(stage, potential, core, nx // 2) for stage in (1, 2)]
    along_z, along_y, beside, pick = [jnp.asarray(m) for m in block_matrices(ZROWS, ny, count)]
    own = turn(potential)
    along_z, along_y, beside, pick = [inside(m) for m in (along_z, along_y, beside, pick)]
    early = (own, along_z, along_y, beside, pick)
    half = count // 2

    halos = [edges(orbitals, c * half, half) for c in range(2)]
    later = halos[1][1]
    halos = [exchange(*halo) for halo in halos]
    first0, on, off = run_stage(
        1, orbitals, *halos[0], tables[0], 0, half, after=(later, *early)
    )
    halos[0] = exchange(on, off)
    first1, on, later = run_stage(1, orbitals, *halos[1], tables[0], half, half)
    halos[1] = exchange(on, later)
    (filtered,) = run_stage(
        2, first0, *halos[0], tables[1], 0, half, orbitals, after=(later,)
    )
    (filtered,) = run_stage(
        2, first1, *halos[1], tables[1], half, half, orbitals, into=filtered
    )
    filtered = inside(lax.all_to_all(filtered, "band", 0, 0))
    low, high = border_lines(filtered, pick)
    up = list(zip(SNAKE[:-1], SNAKE[1:]))
    below = lax.ppermute(high, "band", up)
    above = lax.ppermute(low, "band", [(target, source) for source, target in up])
    on, off = exchange(*border_planes(filtered, low))
    applied = local_stage(filtered, own, along_z, along_y)
    sums = gram(1.0 / cells, filtered, applied)
    totals = total_over_cells(finish(1.0 / cells, (below, above, off, on), beside, *sums))
    return (totals[0], totals[1])


def solution(mesh):
    return jax.shard_map(
        per_device,
        mesh=mesh,
        in_specs=(P("band", "domain", None, None), P("domain", None, None)),
        out_specs=(P("band", None), P("band", None)),
        check_vma=False,
    )
```

```python
import functools

import jax
import jax.numpy as jnp
import ml_dtypes
import numpy as np
from jax import lax
from jax.experimental import pallas as pl
from jax.experimental.pallas import tpu as pltpu
from jax.sharding import PartitionSpec as P

COEFS = (
    -5369.0 / 1800.0,
    12.0 / 7.0,
    -15.0 / 56.0,
    10.0 / 189.0,
    -1.0 / 112.0,
    2.0 / 1925.0,
    -1.0 / 16632.0,
)
CENTER = 8.0
HALF = 5.0
REACH = 6
OUTER = (1.0 / HALF, 2.0 / HALF, 1.0)
SHIFT = (-CENTER / HALF, -2.0 * CENTER / HALF, 0.0)
BF16 = jnp.bfloat16
F32 = jnp.float32
ZROWS = 16
NARROW = REACH // 2
SNAKE = (0, 1, 2, 3, 7, 6, 5, 4)
ROWS = 16
VMEM = 12 * 1024 * 1024


def side_weights(stage):
    return [-0.5 * OUTER[stage - 1] * c for c in COEFS]


def band_matrix(stage, size):
    index = np.arange(size)
    gap = np.abs(index[:, None] - index[None, :])
    weights = np.array([0.0] + side_weights(stage)[1:])
    return np.where(gap <= REACH, weights[np.minimum(gap, REACH)], 0.0)


def split_two(matrix):
    high = matrix.astype(ml_dtypes.bfloat16)
    low = (matrix - high.astype(np.float64)).astype(ml_dtypes.bfloat16)
    return high, low


def stencil_matrices(stage, ny, nz, group):
    high, low = split_two(np.kron(np.eye(group), band_matrix(stage, ny)))
    along_y = np.concatenate([high, low], axis=1)
    along_z = np.concatenate(split_two(band_matrix(stage, nz)), axis=0)
    return jnp.asarray(along_y), jnp.asarray(along_z)


def stage_tables(stage, potential, core, group):
    ny, nz = potential.shape[1:]
    own = OUTER[stage - 1] * (potential - 1.5 * COEFS[0]) + SHIFT[stage - 1]
    own = jnp.where(core == 0, own, own[::-1])
    return (own, *stencil_matrices(stage, ny, nz, group))


def stage_body(stage, unused, orbs, first, at, *refs):
    width = REACH
    c_ref, off_ref, on_ref, v_ref, my_ref, mz_ref = refs[:6]
    refs = refs[6:]
    if stage == 2:
        o_ref = refs[0]
        refs = refs[1:]
    outs = refs[unused:]
    core = this_core()
    nx, ny, nz = v_ref.shape
    group = my_ref.shape[0] // ny

    def given(ref, b, p, rows):
        return ref[b, p + core * (nx - 1 - 2 * p), rows]

    def center(b, p, rows):
        return given(c_ref, first + b, p, rows) if stage == 1 else c_ref[p, b, rows]

    def beyond(b, i, rows):
        if stage == 1:
            return on_ref[b, i + core * (width - 1 - 2 * i), rows]
        return on_ref[width - 1 - i, b, rows]

    def before(b, i, rows):
        if stage == 1:
            return off_ref[b, (width - 1 - i) + core * (2 * i + 1 - width), rows]
        return off_ref[i, b, rows]

    everything = slice(0, ny)
    side = side_weights(stage)

    def orbital(b):
        lines = [center(b, p, everything) for p in range(nx)]
        sides = [jnp.concatenate(lines[q : q + group], axis=0) for q in range(0, nx, group)]
        part = jnp.concatenate(sides, axis=1)
        flat = jnp.concatenate(sides, axis=0)
        z_term = jnp.dot(
            jnp.concatenate([flat, flat], axis=1), mz_ref[...], preferred_element_type=F32
        ).reshape(nx, ny, nz)
        y_term = jnp.dot(
            my_ref[...], jnp.concatenate([part, part], axis=0), preferred_element_type=F32
        )
        y_parts = [
            y_term[:, k * nz : (k + 1) * nz].reshape(group, ny, nz) for k in range(nx // group)
        ]
        results = {}
        for r in range(0, ny, ROWS):
            rows = slice(r, r + ROWS)
            wide = {}
            for p in range(nx):
                wide[p] = center(b, p, rows).astype(F32)
            for i in range(width):
                wide[-1 - i] = before(b, i, rows).astype(F32)
                wide[nx + i] = beyond(b, i, rows).astype(F32)
            for p in range(nx):
                total = (
                    v_ref[p, rows] * wide[p]
                    + z_term[p, rows]
                    + y_parts[p // group][p % group, rows]
                )
                for s in range(1, REACH + 1):
                    near = []
                    for q in (p - s, p + s):
                        near.append(wide[q])
                    total = total + side[s] * sum(near[1:], near[0])
                if stage == 2:
                    total = total - given(o_ref, first + b, p, rows).astype(F32)
                results[p, r] = total.astype(BF16)
        return results

    if stage == 1:
        for b in range(orbs):
            for (p, r), result in orbital(b).items():
                rows = slice(r, r + ROWS)
                outs[0][p, b, rows] = result
                if p >= nx - REACH:
                    outs[1][p - (nx - REACH), b, rows] = result
                if p < REACH:
                    outs[2][p, b, rows] = result
    else:
        for b in range(orbs // 2):
            pair = [orbital(b), orbital(b + orbs // 2)]
            for p in range(nx):
                both = jnp.concatenate(
                    [one[p, r] for one in pair for r in range(0, ny, ROWS)], axis=0
                )
                turned = both.T
                for block, band in enumerate(SNAKE):
                    outs[0][band, p, at + b] = turned[block * ZROWS : (block + 1) * ZROWS]


def iota2(size, dim):
    return lax.broadcasted_iota(jnp.int32, (size, size), dim)


def dot_rows(left, right):
    return lax.dot_general(left, right, (((1,), (1,)), ((), ())), preferred_element_type=F32)


def inside(array):
    return pltpu.with_memory_space_constraint(array, pltpu.VMEM)


def run_stage(stage, field, on, off, tables, first, orbs, orbitals=None, after=(), into=None):
    nx, ny, nz = tables[0].shape
    args = [field, off, on, *tables]
    if stage == 2:
        args.append(orbitals)
        count = orbitals.shape[0]
        out_shape = [pltpu.VMEM((nz // ZROWS, nx, count // 2, ZROWS, 2 * ny), BF16)]
    else:
        out_shape = [pltpu.VMEM((n, orbs, ny, nz), BF16) for n in (nx, REACH, REACH)]
    args = [inside(array) for array in args]
    unused = list(after)
    aliases = {}
    vmem = pl.BlockSpec(memory_space=pltpu.VMEM)
    specs = [vmem] * len(args) + [pl.BlockSpec(memory_space=pl.ANY)] * len(unused)
    if into is not None:
        aliases = {len(args): 0}
        unused = [inside(into)] + unused
        specs.insert(len(args), vmem)
    return pl.pallas_call(
        functools.partial(stage_body, stage, len(unused), orbs, first, first // 2),
        in_specs=specs,
        out_specs=[vmem] * len(out_shape),
        out_shape=out_shape,
        input_output_aliases=aliases,
        compiler_params=pltpu.CompilerParams(vmem_limit_bytes=VMEM),
        cost_estimate=pl.CostEstimate(
            flops=orbs * nx * ny * nz * 1200, bytes_accessed=orbs * nx * ny * nz * 8, transcendentals=0
        ),
        name="stage%d" % stage,
    )(*args, *unused)


def edges_body(first, far, in_ref, on_ref, off_ref):
    own = this_core()
    for core in range(2):

        @pl.when(own == core)
        def _():
            for b in range(on_ref.shape[0]):
                on = [in_ref[first + b, i + far * (1 - core)] for i in range(REACH)]
                off = [in_ref[first + b, i + far * core] for i in range(REACH)]
                for i in range(REACH):
                    on_ref[b, i] = on[i]
                    off_ref[b, i] = off[i]


def edges(orbitals, first, orbs):
    nx, ny, nz = orbitals.shape[1:]
    shape = pltpu.VMEM((orbs, REACH, ny, nz), BF16)
    vmem = pl.BlockSpec(memory_space=pltpu.VMEM)
    return pl.pallas_call(
        functools.partial(edges_body, first, nx - REACH),
        in_specs=[vmem],
        out_specs=[vmem, vmem],
        out_shape=[shape, shape],
        compiler_params=pltpu.CompilerParams(vmem_limit_bytes=VMEM),
        name="edges",
    )(inside(orbitals))


def exchange(on, off):
    count = lax.axis_size("domain")
    pairs = [(i, i ^ 1) for i in range(count)]
    facing = [(i, i + 1) for i in range(1, count - 1, 2)]
    facing += [(target, source) for source, target in facing]
    on = lax.ppermute(on, "domain", pairs)
    off = lax.ppermute(off, "domain", facing)
    return on, off


def this_core():
    return lax.axis_index("domain") % 2


def turn_body(v_ref, out_ref, held_ref):
    core = this_core()
    band = lax.axis_index("band")
    block = jnp.where(band < 4, band, 11 - band)
    nx = v_ref.shape[0]
    for p in range(nx):
        line = v_ref[p + core * (nx - 1 - 2 * p)] - 1.5 * COEFS[0]
        held_ref[p] = jnp.concatenate([line, line], axis=0).T
    for p in range(nx):
        out_ref[p] = held_ref[p, pl.ds(pl.multiple_of(block * ZROWS, ZROWS), ZROWS), :]


def turn(potential):
    nx, ny, nz = potential.shape
    vmem = pl.BlockSpec(memory_space=pltpu.VMEM)
    return pl.pallas_call(
        turn_body,
        in_specs=[vmem],
        out_specs=vmem,
        out_shape=pltpu.VMEM((nx, ZROWS, 2 * ny), F32),
        scratch_shapes=[pltpu.VMEM((nx, nz, 2 * ny), F32)],
        compiler_params=pltpu.CompilerParams(vmem_limit_bytes=VMEM),
        name="turn",
    )(inside(potential))


def block_matrices(nz_block, ny, blocks):
    side = side_weights(3)
    reach = NARROW
    low, high = np.zeros((nz_block, reach)), np.zeros((nz_block, reach))
    for i in range(nz_block):
        for j in range(reach):
            gap = i + reach - j
            if gap <= REACH:
                low[i, j] = side[gap] * (1 if i < reach else 2)
            gap = nz_block - i + j
            if gap <= REACH:
                high[i, j] = side[gap] * (1 if nz_block - 1 - i < reach else 2)
    unit = np.eye(blocks)
    own = split_two(np.kron(unit, band_matrix(3, nz_block)))
    beside = split_two(np.concatenate([np.kron(unit, low), np.kron(unit, high)], axis=1))
    along_z, beside = np.concatenate(own, axis=1), np.concatenate(beside, axis=1)
    twice = np.kron(np.eye(2), band_matrix(3, ny))
    along_y = np.concatenate(split_two(twice), axis=0)
    pick = np.zeros((2, reach, nz_block))
    for j in range(reach):
        pick[0, j, j] = 1
        pick[1, j, nz_block - reach + j] = 1
    pick = np.concatenate([np.kron(unit, pick[0]), np.kron(unit, pick[1])], axis=0)
    return along_z, along_y, beside, pick.astype(ml_dtypes.bfloat16)


def two_planes(ref, s, p):
    pairs, rows, lanes = ref.shape[2:]
    return jnp.concatenate([ref[s, p + i].reshape(pairs * rows, lanes) for i in range(2)], axis=0)


def lines_body(f_ref, pick_ref, low_ref, high_ref):
    bands, nx = f_ref.shape[:2]
    count = low_ref.shape[2]
    for s in range(bands):
        for p in range(0, nx, 2):
            rows = jnp.dot(pick_ref[...], two_planes(f_ref, s, p), preferred_element_type=F32)
            rows = rows.astype(BF16)
            low_ref[s, p // 2] = rows[:count]
            high_ref[s, p // 2] = rows[count:]


def border_lines(filtered, pick):
    bands, nx, pairs, rows, lanes = filtered.shape
    vmem = pl.BlockSpec(memory_space=pltpu.VMEM)
    lines = pltpu.VMEM((bands, nx // 2, pick.shape[0] // 2, lanes), BF16)
    return pl.pallas_call(
        lines_body,
        in_specs=[vmem, vmem],
        out_specs=[vmem] * 2,
        out_shape=[lines, lines],
        compiler_params=pltpu.CompilerParams(vmem_limit_bytes=VMEM),
        name="lines",
    )(filtered, inside(pick))


def planes_body(f_ref, after_ref, on_ref, off_ref):
    bands, nx = f_ref.shape[:2]
    for s in range(bands):
        for p in range(NARROW):
            off_ref[s, p] = f_ref[s, p]
            on_ref[s, p] = f_ref[s, nx - NARROW + p]


def border_planes(filtered, after):
    bands, nx, pairs, rows, lanes = filtered.shape
    vmem = pl.BlockSpec(memory_space=pltpu.VMEM)
    planes = pltpu.VMEM((bands, NARROW, pairs, rows, lanes), BF16)
    return pl.pallas_call(
        planes_body,
        in_specs=[vmem, pl.BlockSpec(memory_space=pl.ANY)],
        out_specs=[vmem] * 2,
        out_shape=[planes, planes],
        compiler_params=pltpu.CompilerParams(vmem_limit_bytes=VMEM),
        name="planes",
    )(filtered, after)


def local_body(f_ref, v_ref, mz_ref, my_ref, out_ref):
    bands, nx, pairs, rows, lanes = f_ref.shape
    side = side_weights(3)
    for s in range(bands):
        z_terms, y_terms = [], []
        for p in range(0, nx, 4):
            data = jnp.concatenate([two_planes(f_ref, s, p + i) for i in (0, 2)], axis=1)
            term = jnp.dot(
                mz_ref[...], jnp.concatenate([data, data], axis=0), preferred_element_type=F32
            )
            for i in range(2):
                half = term[:, i * lanes : (i + 1) * lanes].reshape(2, pairs, rows, lanes)
                z_terms += [half[0], half[1]]
        for p in range(0, nx, 2):
            data = two_planes(f_ref, s, p)
            term = jnp.dot(
                jnp.concatenate([data, data], axis=1), my_ref[...], preferred_element_type=F32
            ).reshape(2, pairs, rows, lanes)
            y_terms += [term[0], term[1]]
        results = {}
        for q in range(pairs):
            wide = [f_ref[s, p, q].astype(F32) for p in range(nx)]
            for p in range(nx):
                total = v_ref[p] * wide[p] + z_terms[p][q] + y_terms[p][q]
                for gap in range(1, REACH + 1):
                    near = [wide[other] for other in (p - gap, p + gap) if 0 <= other < nx]
                    if near:
                        total = total + side[gap] * sum(near[1:], near[0])
                results[p, q] = total.astype(BF16)
        for (p, q), result in results.items():
            out_ref[s, p, q] = result


def local_stage(filtered, own, along_z, along_y):
    vmem = pl.BlockSpec(memory_space=pltpu.VMEM)
    args = [inside(array) for array in (filtered, own, along_z, along_y)]
    return pl.pallas_call(
        local_body,
        in_specs=[vmem] * len(args),
        out_specs=vmem,
        out_shape=pltpu.VMEM(filtered.shape, BF16),
        compiler_params=pltpu.CompilerParams(vmem_limit_bytes=VMEM),
        cost_estimate=pl.CostEstimate(flops=10**9, bytes_accessed=2**22, transcendentals=0),
        name="local",
    )(*args)


def orbital_rows(block):
    count, rows, lanes = block.shape
    half = lanes // 2
    change = iota2(lanes, 0) == (iota2(lanes, 1) + half) % lanes
    change = change.astype(F32).astype(BF16)
    block = jnp.swapaxes(block, 0, 1)
    changed = jnp.dot(block.reshape(rows * count, lanes), change, preferred_element_type=F32)
    changed = changed.astype(BF16).reshape(rows, count, lanes)
    first = lax.broadcasted_iota(jnp.int32, (count, lanes), 1) < half
    parts = []
    for z in range(0, rows, 2):
        even = jnp.where(first, block[z], changed[z + 1])
        odd = jnp.where(first, changed[z], block[z + 1])
        parts.append(jnp.concatenate([even, odd], axis=0))
    return [jnp.concatenate(parts[i : i + 2], axis=1) for i in range(0, len(parts), 2)]


def natural_rows(square, pairs):
    size = square.shape[0]
    four = pairs // 2
    parts = []
    for row in range(0, size, four):
        band, chunk, half = row // (4 * four), (row // (2 * four)) % 2, (row // four) % 2
        start = half * (size // 2) + band * pairs + chunk * four
        parts.append(square[start : start + four])
    return jnp.concatenate(parts, axis=0)


def gram_body(scale, f_ref, a_ref, corr_ref, total_ref, right_ref):
    bands, nx, pairs, rows, lanes = f_ref.shape
    count = bands * pairs

    def block(p, total):
        right = orbital_rows(f_ref[:, p].reshape(count, rows, lanes))
        left = orbital_rows(a_ref[:, p].reshape(count, rows, lanes))
        for i, (one, other) in enumerate(zip(right, left)):
            right_ref[p, i] = one
            total = total + dot_rows(jnp.concatenate([one, other], axis=0), one)
        return total

    total = jnp.zeros((4 * count, 2 * count), F32)
    for p in range(nx):
        total = block(p, total)
    total_ref[...] = total[2 * count :]
    corr = natural_rows(total[: 2 * count] * scale, pairs).T
    corr_ref[...] = natural_rows(corr, pairs)


def gram(scale, filtered, applied):
    bands, nx, pairs, rows, lanes = filtered.shape
    size = 2 * bands * pairs
    vmem = pl.BlockSpec(memory_space=pltpu.VMEM)
    return pl.pallas_call(
        functools.partial(gram_body, scale),
        in_specs=[vmem, vmem],
        out_specs=[vmem] * 3,
        out_shape=[
            pltpu.VMEM((size, size), F32),
            pltpu.VMEM((size, size), F32),
            pltpu.VMEM((nx, rows // 4, size, 2 * lanes), BF16),
        ],
        compiler_params=pltpu.CompilerParams(vmem_limit_bytes=3 * VMEM),
        cost_estimate=pl.CostEstimate(flops=10**9, bytes_accessed=2**22, transcendentals=0),
        name="gram",
    )(inside(filtered), inside(applied))


def finish_body(
    scale,
    low_ref,
    high_ref,
    off_ref,
    on_ref,
    beside_ref,
    corr_ref,
    total_ref,
    right_ref,
    out_ref,
    cross_ref,
):
    bands, width, pairs, rows, lanes = off_ref.shape
    nx = right_ref.shape[0]
    count = bands * pairs
    side = side_weights(3)
    for s in range(bands):
        z_terms = []
        for p in range(0, nx, 4):
            halo = jnp.concatenate(
                [
                    jnp.concatenate([low_ref[s, p // 2 + i], high_ref[s, p // 2 + i]], axis=0)
                    for i in range(2)
                ],
                axis=1,
            )
            term = jnp.dot(
                beside_ref[...],
                jnp.concatenate([halo, halo], axis=0),
                preferred_element_type=F32,
            )
            for i in range(2):
                half = term[:, i * lanes : (i + 1) * lanes].reshape(2, pairs, rows, lanes)
                z_terms += [half[0], half[1]]
        for q in range(pairs):
            off = [off_ref[s, i, q].astype(F32) for i in range(width)]
            on = [on_ref[s, width - 1 - i, q].astype(F32) for i in range(width)]
            for p in range(nx):
                total = z_terms[p][q]
                for beyond, depth in ((off, p), (on, nx - 1 - p)):
                    weight = 2.0 if depth >= width else 1.0
                    for i in range(width):
                        if depth + i + 1 <= REACH:
                            total = total + (weight * side[depth + i + 1]) * beyond[i]
                cross_ref[s, p, q] = total.astype(BF16)

    def block(p, total):
        left = orbital_rows(cross_ref[:, p].reshape(count, rows, lanes))
        for i, one in enumerate(left):
            total = total + dot_rows(one, right_ref[p, i])
        return total

    proj = total_ref[...]
    for p in range(nx):
        proj = block(p, proj)
    proj = natural_rows((0.5 * scale) * (proj + proj.T), pairs).T
    proj = natural_rows(proj, pairs)
    size = 2 * pairs
    for band in range(bands):
        out_ref[band, 0] = corr_ref[band * size : (band + 1) * size]
        out_ref[band, 1] = proj[band * size : (band + 1) * size]


def finish(scale, halos, beside, corr, total, right):
    bands, _, pairs, rows, lanes = halos[2].shape
    vmem = pl.BlockSpec(memory_space=pltpu.VMEM)
    args = [inside(array) for array in (*halos, beside, corr, total, right)]
    return pl.pallas_call(
        functools.partial(finish_body, scale),
        in_specs=[vmem] * len(args),
        out_specs=vmem,
        out_shape=jax.ShapeDtypeStruct((bands, 2, 2 * pairs, 2 * bands * pairs), F32),
        scratch_shapes=[pltpu.VMEM((bands, right.shape[0], pairs, rows, lanes), BF16)],
        compiler_params=pltpu.CompilerParams(vmem_limit_bytes=3 * VMEM),
        name="finish",
    )(*args)


def swap(value, partner):
    pairs = []
    for b in range(8):
        for d in range(16):
            x, y, z, core = partner(b % 4, (b // 4) * 2 + d // 8, (d // 2) % 4, d % 2)
            pairs.append((b * 16 + d, ((y // 2) * 4 + x) * 16 + (y % 2) * 8 + z * 2 + core))
    return lax.ppermute(value, ("band", "domain"), pairs)


def total_over_cells(partial):
    domains = lax.axis_size("domain")
    half = domains // 2
    groups = [
        [band * domains + y * half + rest for band in range(8) for y in range(2)]
        for rest in range(half)
    ]
    pieces = jnp.broadcast_to(partial[:, None], (8, 2) + partial.shape[1:])
    pieces = pieces.reshape((16,) + partial.shape[1:])
    value = lax.all_to_all(pieces, ("band", "domain"), 0, 0, axis_index_groups=groups).sum(0)
    value = value + swap(value, lambda x, y, z, c: (x, y, z, 1 - c))
    value = value + swap(value, lambda x, y, z, c: (x, y, z ^ 3, c))
    value = value + swap(value, lambda x, y, z, c: (x, y, z ^ 1, c))
    return value


def per_device(orbitals, potential):
    count, nx, ny, nz = orbitals.shape
    cells = float(nx * lax.axis_size("domain") * ny * nz)
    core = this_core()
    tables = [stage_tables(stage, potential, core, nx // 2) for stage in (1, 2)]
    along_z, along_y, beside, pick = [jnp.asarray(m) for m in block_matrices(ZROWS, ny, count)]
    own = turn(potential)
    along_z, along_y, beside, pick = [inside(m) for m in (along_z, along_y, beside, pick)]
    early = (own, along_z, along_y, beside, pick)
    half = count // 2

    halos = [edges(orbitals, c * half, half) for c in range(2)]
    later = halos[1][1]
    halos = [exchange(*halo) for halo in halos]
    first0, on, off = run_stage(
        1, orbitals, *halos[0], tables[0], 0, half, after=(later, *early)
    )
    halos[0] = exchange(on, off)
    first1, on, later = run_stage(1, orbitals, *halos[1], tables[0], half, half)
    halos[1] = exchange(on, later)
    (filtered,) = run_stage(
        2, first0, *halos[0], tables[1], 0, half, orbitals, after=(later,)
    )
    (filtered,) = run_stage(
        2, first1, *halos[1], tables[1], half, half, orbitals, into=filtered
    )
    filtered = inside(lax.all_to_all(filtered, "band", 0, 0))
    low, high = border_lines(filtered, pick)
    up = list(zip(SNAKE[:-1], SNAKE[1:]))
    below = lax.ppermute(high, "band", up)
    above = lax.ppermute(low, "band", [(target, source) for source, target in up])
    on, off = exchange(*border_planes(filtered, low))
    applied = local_stage(filtered, own, along_z, along_y)
    sums = gram(1.0 / cells, filtered, applied)
    totals = total_over_cells(finish(1.0 / cells, (below, above, off, on), beside, *sums))
    return (totals[0], totals[1])


def solution(mesh):
    return jax.shard_map(
        per_device,
        mesh=mesh,
        in_specs=(P("band", "domain", None, None), P("domain", None, None)),
        out_specs=(P("band", None), P("band", None)),
        check_vma=False,
    )
```
